512 devices in a mesh: dp: 8 (over z), seq: 64 (over y, x, core).
Axes of the slice: x: 4, y: 8, z: 8, core: 2. Of those that a mesh axis runs over, the one named last changes fastest.
Arguments:
- tokens: bfloat16 [8, 8192, 1280], P('dp', 'seq'), may hold values from -6 to 6
- place: int32 [64, 128], P('seq'), may hold values from 0 to 127, each once within a row
- kernel: float32 [27, 1280], replicated, may hold values from -1.25 to 1.25
- proj_weight: bfloat16 [1280, 3840], P('seq'), may hold values from -0.15625 to 0.15625
- d_projected: bfloat16 [8, 8192, 3840], P('dp', 'seq'), may hold values from -6 to 6
Outputs:
- projected: bfloat16 [8, 8192, 3840], P('dp', 'seq')
- d_tokens: bfloat16 [8, 8192, 1280], P('dp', 'seq')
- d_kernel: float32 [27, 1280], replicated
The draws below stay inside these ranges and needn't reach their ends.
Inputs may be any that keep to these rules, and one draw needn't show every extreme that they name: Each row of place holds every number 0 to 127 once.
All inputs are finite; a program needn't handle non-finite values.
Results may differ from the reference program's by a relative error of at most 0.005.
Values may be sent and summed in bfloat16 or wider, within the bound.
No kernel may reach another device: no remote copies, remote signals or barrier semaphores. Data moves between devices by JAX's collectives and lax.ppermute only.
A program may use at most 128 MiB of HBM per device.

```python
import jax
import jax.numpy as jnp
from jax import lax

D = 1280
INLINE = 8
CROSS = 8
TOK_DEV = 128
QKV = 3840
VOLUMES = 8
SEQLEN = 8192
DEPTH = 128
N_SEQ = 64


def block_scale(own_key, extent, split, least, top_value):
    def one(axis_at, shards_of):
        steps = jax.random.uniform(jax.random.fold_in(jax.random.fold_in(own_key, 6), axis_at), (shards_of,), jnp.float32, least / len(split), top_value / len(split))
        return jnp.repeat(jnp.exp(steps), extent[axis_at] // shards_of).reshape((-1,) + (1,) * (len(extent) - axis_at - 1))

    level = one(*split[0])
    for cut in split[1:]:
        level = level * one(*cut)
    return level


def centred(stream_key, extent, scale, most, cuts=(), kind=jnp.bfloat16):
    drawn = jax.random.normal(stream_key, extent, jnp.float32) * scale
    if len(cuts) > 0:
        drawn = block_scale(stream_key, extent, cuts, -0.22, 0.18) * drawn
    return jnp.clip(drawn, min=-most, max=most).astype(kind)


def setup_inputs(seed: int = 0) -> dict:
    arg_keys = jax.random.split(jax.random.key(seed), 6)
    tokens = centred(arg_keys[0], (VOLUMES, SEQLEN, D), 1.0, 6.0, ((0, 8), (1, 64)))
    place = jax.vmap(lambda own: jax.random.permutation(own, TOK_DEV))(jax.random.split(arg_keys[1], N_SEQ)).reshape((N_SEQ, TOK_DEV)).astype(jnp.int32)
    kernel = centred(arg_keys[2], (27, D), 27 ** -0.5, 1.25, (), jnp.float32)
    proj_weight = centred(arg_keys[3], (D, QKV), D ** -0.5, 0.15625, ((0, 64),))
    d_projected = centred(arg_keys[4], (VOLUMES, SEQLEN, QKV), 1.0, 6.0, ((0, 8), (1, 64)))
    return dict(tokens=tokens, place=place, kernel=kernel, proj_weight=proj_weight, d_projected=d_projected)


def grid_index(place):
    group = TOK_DEV // N_SEQ
    scan = jnp.arange(SEQLEN, dtype=jnp.int32)
    device = scan // TOK_DEV
    within = scan % TOK_DEV
    brick = within // group
    slot = device * group + within % group
    return (brick * TOK_DEV + place[brick, slot]).astype(jnp.int32)


def to_grid(rows, target):
    width = rows.shape[-1]
    grid = jnp.zeros((SEQLEN, width), rows.dtype).at[target].set(rows)
    return grid.reshape(DEPTH, INLINE, CROSS, width)


def to_scan(grid, target):
    return grid.reshape(SEQLEN, grid.shape[-1])[target]


def padded(grid):
    return jnp.pad(grid, ((1, 1), (1, 1), (1, 1), (0, 0)))


def window(field, start_z, start_i, start_c):
    return field[start_z:start_z + DEPTH, start_i:start_i + INLINE, start_c:start_c + CROSS].astype(jnp.float32)


def one_volume(tokens, d_projected, target, kernel, proj_weight):
    grid_x = to_grid(tokens, target)
    pad_x = padded(grid_x)
    conv = jnp.zeros(grid_x.shape, jnp.float32)
    for offset in range(27):
        conv = conv + kernel[offset] * window(pad_x, offset // 9, (offset // 3) % 3, offset % 3)
    grid_y = (grid_x.astype(jnp.float32) + conv).astype(jnp.bfloat16)
    rows_y = to_scan(grid_y, target)
    projected = jnp.dot(rows_y, proj_weight, preferred_element_type=jnp.float32).astype(jnp.bfloat16)
    d_y = jnp.dot(d_projected, proj_weight.T, preferred_element_type=jnp.float32).astype(jnp.bfloat16)
    grid_d = to_grid(d_y, target)
    pad_d = padded(grid_d)
    back = grid_d.astype(jnp.float32)
    d_kernel = []
    for offset in range(27):
        dz, di, dc = offset // 9, (offset // 3) % 3, offset % 3
        back = back + kernel[offset] * window(pad_d, 2 - dz, 2 - di, 2 - dc)
        d_kernel.append(jnp.sum(grid_d.astype(jnp.float32) * window(pad_x, dz, di, dc), axis=(0, 1, 2)))
    d_tokens = to_scan(back.astype(jnp.bfloat16), target)
    return projected, d_tokens, jnp.stack(d_kernel)


def reference(tokens, place, kernel, proj_weight, d_projected):
    target = grid_index(place)

    def step(pair):
        return one_volume(pair[0], pair[1], target, kernel, proj_weight)

    projected, d_tokens, d_kernel = lax.map(step, (tokens, d_projected))
    return projected, d_tokens, jnp.sum(d_kernel, axis=0)
```

```python
import functools

import jax
import jax.numpy as jnp
import numpy as np
from jax import lax
from jax.experimental import pallas as pl
from jax.experimental.pallas import tpu as pltpu
from jax.sharding import Mesh
from jax.sharding import PartitionSpec as P

NY, NX, NC = 8, 4, 2
CHIPS = NY * NX
LAYER = 64
BF16, F32 = jnp.bfloat16, jnp.float32


def swap(value):
    return lax.ppermute(value, "c", [(0, 1), (1, 0)])


def in_order(core, own, other, axis):
    first = jnp.where(core == 0, own, other)
    second = jnp.where(core == 0, other, own)
    return jnp.concatenate([first, second], axis=axis)


def half(value, core):
    width = value.shape[-1] // 2
    return lax.dynamic_slice_in_dim(value, core * width, width, axis=value.ndim - 1)


def spread(value, axis, size):
    return lax.all_to_all(
        jnp.broadcast_to(value[None], (size, *value.shape)), axis, 0, 0, tiled=True
    )


def shift(value, axis, size, step):
    return lax.ppermute(value, axis, [(i, (i + step) % size) for i in range(size)])


def weight_pieces(block):
    rows = block.shape[0] // 2
    up, down = block, block
    pieces = [block]
    for _ in range(3):
        up, down = shift(up, "y", NY, 1), shift(down, "y", NY, -1)
        pieces += [up, down]
    pieces += [shift(up[:rows], "y", NY, 1), shift(down[rows:], "y", NY, -1)]
    return pieces


def assemble(y_ref, pieces, weight, sems):
    rows = pieces[0].shape[0]
    places = [(0, 0), (-1, 0), (1, 0), (-2, 0), (2, 0), (-3, 0), (3, 0), (4, 0), (4, rows // 2)]
    copies = []
    for i, (piece, (step, skip)) in enumerate(zip(pieces, places)):
        at = lax.rem(y_ref[0] + step + NY, NY) * rows + skip
        at = pl.multiple_of(at, 16)
        copies.append(
            pltpu.make_async_copy(piece, weight.at[pl.ds(at, piece.shape[0])], sems.at[i])
        )
    for copy in copies:
        copy.start()
    return copies


def weight_call(body, pieces, out_shape, vmem):
    columns = pieces[0].shape[1]
    total = pieces[0].shape[0] * NY
    return pl.pallas_call(
        body,
        out_shape=out_shape,
        in_specs=[pl.BlockSpec(memory_space=pltpu.SMEM), pl.BlockSpec(memory_space=pltpu.VMEM)]
        + [pl.BlockSpec(memory_space=pl.ANY)] * len(pieces),
        scratch_shapes=[
            pltpu.VMEM((total, columns), BF16),
            pltpu.SemaphoreType.DMA((len(pieces),)),
        ],
        compiler_params=pltpu.CompilerParams(vmem_limit_bytes=vmem),
        cost_estimate=pl.CostEstimate(
            flops=2 * 256 * total * columns, bytes_accessed=8_000_000, transcendentals=0
        ),
    )


def back_kernel(where_ref, rows_ref, *refs):
    pieces, (keep_ref, send_ref, weight, sems) = refs[:9], refs[9:]
    for copy in assemble(where_ref, pieces, weight, sems):
        copy.wait()
    width = keep_ref.shape[1]
    core = where_ref[1]
    for out, which in ((send_ref, 1 - core), (keep_ref, core)):
        for at, size in ((0, 256), (256, 256), (512, 128)):
            start = pl.multiple_of(which * width + at, 128)
            out[:, at : at + size] = lax.dot_general(
                rows_ref[...],
                weight[pl.ds(start, size), :],
                (((1,), (1,)), ((), ())),
                preferred_element_type=F32,
            )


def forward_kernel(where_ref, rows_ref, *refs):
    pieces, (out_ref, weight, sems) = refs[:9], refs[9:]
    for copy in assemble(where_ref, pieces, weight, sems):
        copy.wait()
    for at in range(0, out_ref.shape[1], 384):
        out_ref[:, at : at + 384] = jnp.dot(
            rows_ref[...], weight[:, at : at + 384], preferred_element_type=F32
        ).astype(BF16)


def cells_kernel(cell_ref, rows_ref, out_ref):
    count = rows_ref.shape[0]
    pick = lax.broadcasted_iota(jnp.int32, (count, count), 0) == cell_ref[...]
    pick = jnp.where(pick, 1.0, 0.0).astype(BF16)
    out_ref[...] = jnp.dot(pick, rows_ref[...], preferred_element_type=F32).astype(BF16)


def to_cells(rows, cell_row):
    return pl.pallas_call(
        cells_kernel,
        out_shape=jax.ShapeDtypeStruct(rows.shape, BF16),
        in_specs=[pl.BlockSpec(memory_space=pltpu.VMEM)] * 2,
        out_specs=pl.BlockSpec(memory_space=pltpu.VMEM),
    )(cell_row, rows)


def fill(before_ref, cells_ref, after_ref, field):
    parts = (before_ref[...], cells_ref[...], after_ref[...])
    lanes = cells_ref.shape[1]
    wide = jnp.concatenate([p.astype(F32) for p in parts], axis=0)
    wide = wide.reshape(6 * 8, 8, lanes)
    column = lax.broadcasted_iota(jnp.int32, wide.shape, 1)
    lower = jnp.where(column == 0, 0.0, jnp.roll(wide, 1, axis=1))
    upper = jnp.where(column == 7, 0.0, jnp.roll(wide, -1, axis=1))
    zero = jnp.zeros((6, 1, 8, lanes), F32)
    for s, value in enumerate((lower, wide, upper)):
        field[s, :, 0:1] = zero
        field[s, :, 9:10] = zero
        field[s, :, 1:9] = value.reshape(6, 8, 8, lanes)


def conv_kernel(cell_ref, kernel_ref, before_ref, cells_ref, after_ref, out_ref, field):
    fill(before_ref, cells_ref, after_ref, field)
    count, lanes = cells_ref.shape
    layers = []
    for z in range(4):
        total = jnp.zeros((8, 8, lanes), F32)
        for o in range(27):
            dz, di, dc = o // 9, o // 3 % 3, o % 3
            total = total + kernel_ref[o : o + 1, :][None] * field[dc, z + dz, di : di + 8]
        layers.append(total)
    conv = jnp.stack(layers).reshape(count, lanes)
    result = (cells_ref[...].astype(F32) + conv).astype(BF16)
    pick = lax.broadcasted_iota(jnp.int32, (count, count), 1) == cell_ref[...]
    pick = jnp.where(pick, 1.0, 0.0).astype(BF16)
    out_ref[...] = jnp.dot(pick, result, preferred_element_type=F32).astype(BF16)


def tall(rows, lanes=128):
    return pl.BlockSpec((rows, lanes), lambda t: (0, t))


def conv_rows(cells, before, after, kernel, cell_column):
    count, width = cells.shape
    return pl.pallas_call(
        conv_kernel,
        out_shape=jax.ShapeDtypeStruct(cells.shape, BF16),
        grid=(width // 128,),
        in_specs=[
            pl.BlockSpec((count, 1), lambda t: (0, 0)),
            tall(kernel.shape[0]),
            tall(LAYER),
            tall(count),
            tall(LAYER),
        ],
        out_specs=tall(count),
        scratch_shapes=[pltpu.VMEM((3, 6, 10, 8, 128), F32)],
    )(cell_column, kernel, before, cells, after)


def grad_kernel(grad_ref, before_ref, cells_ref, after_ref, out_ref, field):
    fill(before_ref, cells_ref, after_ref, field)
    lanes = cells_ref.shape[1]
    grad = grad_ref[...].astype(F32).reshape(4, 8, 8, lanes)
    sums = []
    for o in range(27):
        dz, di, dc = o // 9, o // 3 % 3, o % 3
        part = grad * field[dc, dz : dz + 4, di : di + 8]
        sums.append(jnp.sum(part.reshape(32, 8, lanes), axis=0))
    sums += [jnp.zeros((8, lanes), F32)] * 5
    out_ref[...] = jnp.sum(jnp.stack(sums), axis=1)


def kernel_grad(grad, cells, before, after):
    count, width = cells.shape
    return pl.pallas_call(
        grad_kernel,
        out_shape=jax.ShapeDtypeStruct((32, width), F32),
        grid=(width // 128,),
        in_specs=[tall(count), tall(LAYER), tall(count), tall(LAYER)],
        out_specs=tall(32),
        scratch_shapes=[pltpu.VMEM((3, 6, 10, 8, 128), F32)],
    )(grad, before, cells, after)


def to_bricks(rows):
    width = rows.shape[-1]
    sent = rows.reshape(2, CHIPS, 4, width).transpose(1, 0, 2, 3).reshape(CHIPS, 8, width)
    return lax.all_to_all(sent, ("y", "x"), 0, 0, tiled=True).reshape(CHIPS * 8, width)


def to_scan(rows):
    width = rows.shape[-1]
    landed = lax.all_to_all(rows.reshape(CHIPS, 8, width), ("y", "x"), 0, 0, tiled=True)
    return landed.reshape(CHIPS, 2, 4, width).transpose(1, 0, 2, 3).reshape(2, 4 * CHIPS, width)


def faces(cells):
    up = [(i, i + 1) for i in range(CHIPS - 1)]
    down = [(j, i) for i, j in up]
    before = lax.ppermute(cells[-LAYER:], ("y", "x"), up)
    after = lax.ppermute(cells[:LAYER], ("y", "x"), down)
    return before, after


def shards(planes, tokens, place, kernel, proj_weight, d_projected):
    core = lax.axis_index("c")
    rows_x, rows_d = tokens[0], d_projected[0]
    where = jnp.stack([lax.axis_index("y"), core]).astype(jnp.int32)

    places = in_order(core, place, swap(place), 0)
    cell = places.reshape(2, CHIPS, 2, 2) + jnp.array([0, 128], jnp.int32)[:, None, None, None]
    cell = cell.transpose(1, 2, 0, 3).reshape(4 * CHIPS * 2)
    cell_row, cell_column = cell[None, :], cell[:, None]

    block = in_order(core, half(proj_weight, core), swap(half(proj_weight, 1 - core)), 0)
    block = spread(block, "x", NX).reshape(NX * block.shape[0], block.shape[1])
    pieces = weight_pieces(block)

    d_pair = in_order(core, half(rows_d, core), swap(half(rows_d, 1 - core)), 0)
    x_pair = in_order(core, half(rows_x, core)[None], swap(half(rows_x, 1 - core))[None], 0)
    kern = half(kernel, core)

    cells_x = to_cells(to_bricks(x_pair), cell_row)
    before_x, after_x = faces(cells_x)
    rows_y = conv_rows(cells_x, before_x, after_x, kern, cell_column)
    y_half = to_scan(rows_y)
    y_full = in_order(core, y_half, swap(y_half), 2)
    y_full = y_full.reshape(-1, y_full.shape[-1])

    count, width = y_full.shape
    part = jax.ShapeDtypeStruct((count, width // 2), F32)
    keep, send = weight_call(back_kernel, pieces, (part, part), 40 << 20)(where, d_pair, *pieces)
    d_y = (keep + swap(send)).astype(BF16)
    cells_d = to_cells(to_bricks(d_y.reshape(2, count // 2, width // 2)), cell_row)
    before_d, after_d = faces(cells_d)
    partial_value = kernel_grad(cells_d, cells_x, before_x, after_x)
    back = conv_rows(cells_d, before_d, after_d, kern[::-1], cell_column)
    d_half = to_scan(back)
    d_own = lax.dynamic_index_in_dim(d_half, core, 0, keepdims=False)
    d_other = swap(lax.dynamic_index_in_dim(d_half, 1 - core, 0, keepdims=False))
    d_tokens = in_order(core, d_own, d_other, 1)

    tiles = partial_value.reshape(4, 8, 5, 128).transpose(0, 2, 1, 3)
    tiles = jnp.sum(lax.all_to_all(tiles, "x", 0, 0, tiled=True).reshape(NX, 5, 8, 128), axis=0)
    tiles = jnp.sum(spread(tiles, "y", NY), axis=0)
    if planes > 1:
        tiles = jnp.sum(spread(tiles, "z", planes), axis=0)
    tiles = spread(tiles, ("x", "c"), NX * NC).reshape(NX, NC, 5, 8, 128)
    d_kernel = tiles.transpose(0, 3, 1, 2, 4).reshape(32, 1280)[: kernel.shape[0]]

    columns = pieces[0].shape[1]
    out = jax.ShapeDtypeStruct((count, columns), BF16)
    p_pair = weight_call(forward_kernel, pieces, out, 40 << 20)(where, y_full, *pieces)
    p_pair = p_pair.reshape(2, count // 2, columns)
    p_own = lax.dynamic_index_in_dim(p_pair, core, 0, keepdims=False)
    p_other = swap(lax.dynamic_index_in_dim(p_pair, 1 - core, 0, keepdims=False))
    projected = in_order(core, p_own, p_other, 1)
    return projected[None], d_tokens[None], d_kernel


def solution(mesh):
    planes = mesh.shape["dp"]
    devices = np.asarray(mesh.devices).reshape(planes, NY, NX, NC)
    grid = Mesh(devices, ("z", "y", "x", "c"))
    seq = ("y", "x", "c")
    return jax.shard_map(
        functools.partial(shards, planes),
        mesh=grid,
        in_specs=(P("z", seq, None), P(seq, None), P(), P(seq, None), P("z", seq, None)),
        out_specs=(P("z", seq, None), P("z", seq, None), P()),
        check_vma=False,
    )
```

```python
import functools

import jax
import jax.numpy as jnp
import numpy as np
from jax import lax
from jax.experimental import pallas as pl
from jax.experimental.pallas import tpu as pltpu
from jax.sharding import Mesh
from jax.sharding import PartitionSpec as P

NY, NX, NC = 8, 4, 2
CHIPS = NY * NX
TOK = 128
LAYER = 64
GROUP = 20
BF16, F32 = jnp.bfloat16, jnp.float32
VMEM = pl.BlockSpec(memory_space=pltpu.VMEM)
SMEM = pl.BlockSpec(memory_space=pltpu.SMEM)
AWAY = pl.BlockSpec(memory_space=pltpu.HBM)


def swap(value):
    return lax.ppermute(value, "c", [(0, 1), (1, 0)])


def spread(value, axis, size):
    return lax.all_to_all(
        jnp.broadcast_to(value[None], (size, *value.shape)), axis, 0, 0, tiled=True
    )


def shift(value, axis, size, step):
    return lax.ppermute(value, axis, [(i, (i + step) % size) for i in range(size)])


def after(value, *others):
    return lax.optimization_barrier((value, *others))[0]


def params(vmem=None):
    return pltpu.CompilerParams(vmem_limit_bytes=vmem)


ROWS = NX * GROUP
CUT = 48
PIECES = [(s, 0, ROWS) for s in (0, -1, 1, -2, 2, -3, 3)] + [(4, 0, CUT), (4, CUT, ROWS - CUT)]


def ring(up, down):
    return shift(up, "y", NY, 1), shift(down, "y", NY, -1)


def assemble(where_ref, arrays, weight, sems, more):
    copies = [
        pltpu.make_async_copy(source, target, sems.at[len(PIECES) + i])
        for i, (source, target) in enumerate(more)
    ]
    for i, (step, skip, rows) in enumerate(PIECES):
        row = pl.multiple_of(lax.rem(where_ref[0] + step + NY, NY) * ROWS + skip, 16)
        copies.append(
            pltpu.make_async_copy(arrays[i], weight.at[pl.ds(row, rows)], sems.at[i])
        )
    for copy in copies:
        copy.start()
    for copy in copies:
        copy.wait()


def one_hot(hit):
    return jnp.where(hit, 1.0, 0.0).astype(BF16)


def pick_rows(source, count, value):
    shape = (count, value.shape[0])
    hit = lax.broadcasted_iota(jnp.int32, shape, 1) == source(
        lax.broadcasted_iota(jnp.int32, shape, 0)
    )
    return jnp.dot(one_hot(hit), value, preferred_element_type=F32).astype(BF16)


def stacked_row(core):
    def source(row):
        block = lax.shift_right_logical(row, 2) & 1
        at = lax.shift_left(lax.shift_right_logical(row, 3), 2) + (row & 3)
        return at + jnp.where(block == core, 0, TOK)

    return source


def landed_row(block):
    def source(row):
        return lax.shift_left(lax.shift_right_logical(row, 2), 3) + (row & 3) + block * 4

    return source


def both_rows(core):
    def source(row):
        block = jnp.where(row < TOK, core, 1 - core)
        return landed_row(block)(row & (TOK - 1))

    return source


def back_kernel(where_ref, y_ref, own_ref, other_ref, *refs):
    arrays, (out_ref, whole_ref, weight, sems, rows) = refs[: len(PIECES)], refs[len(PIECES) :]
    more = [(own_ref, rows.at[0:TOK]), (other_ref, rows.at[TOK:])]
    assemble(where_ref, arrays, weight, sems, more)
    whole = pltpu.make_async_copy(weight, whole_ref, sems.at[len(PIECES) + 2])
    whole.start()
    width = y_ref.shape[1]
    out_ref[:, 0:width] = y_ref[...]
    for at, size in ((0, 256), (256, 256), (512, 128)):
        part = lax.dot_general(
            rows[...],
            weight[at : at + size, :],
            (((1,), (1,)), ((), ())),
            preferred_element_type=F32,
        ).astype(BF16)
        out_ref[:, width + at : width + at + size] = pick_rows(
            stacked_row(where_ref[1]), part.shape[0], part
        )
    whole.wait()


def back_rows(where, rows_y, own, other, arrays):
    columns = own.shape[1]
    return pl.pallas_call(
        back_kernel,
        out_shape=(
            jax.ShapeDtypeStruct((2 * TOK, 2 * NY * ROWS), BF16),
            jax.ShapeDtypeStruct((NY * ROWS, columns), BF16),
        ),
        in_specs=[SMEM, VMEM] + [AWAY] * (2 + len(arrays)),
        out_specs=(VMEM, AWAY),
        scratch_shapes=[
            pltpu.VMEM((NY * ROWS, columns), BF16),
            pltpu.SemaphoreType.DMA((len(PIECES) + 3,)),
            pltpu.VMEM((2 * TOK, columns), BF16),
        ],
        compiler_params=params(60 << 20),
    )(where, rows_y, own, other, *arrays)


def project_kernel(where_ref, landed_ref, whole_ref, keep_ref, send_ref, weight, sem):
    copy = pltpu.make_async_copy(whole_ref, weight, sem)
    copy.start()
    landed = landed_ref[:, 0 : weight.shape[0]]
    rows = pick_rows(both_rows(where_ref[1]), landed.shape[0], landed)
    copy.wait()
    for at in range(0, weight.shape[1], 768):
        part = jnp.dot(rows, weight[:, at : at + 768], preferred_element_type=F32)
        keep_ref[:, at : at + 768] = part[0:TOK]
        send_ref[:, at : at + 768] = part[TOK:]


def project(where, landed, whole):
    out = jax.ShapeDtypeStruct((TOK, whole.shape[1]), F32)
    return pl.pallas_call(
        project_kernel,
        out_shape=(out, out),
        in_specs=[SMEM, VMEM, AWAY],
        out_specs=(VMEM, VMEM),
        scratch_shapes=[pltpu.VMEM(whole.shape, BF16), pltpu.SemaphoreType.DMA],
        compiler_params=params(60 << 20),
        cost_estimate=pl.CostEstimate(
            flops=4 * TOK * whole.size, bytes_accessed=20_000_000, transcendentals=0
        ),
    )(where, landed, whole)


def chosen(channel_ref, width, dtype=BF16):
    shape = (width, channel_ref.shape[1])
    hit = lax.broadcasted_iota(jnp.int32, shape, 0) == channel_ref[...]
    return jnp.where(hit, 1.0, 0.0).astype(dtype)


def select_kernel(own_ref, other_ref, rows_ref, place_ref, kernel_ref, x_ref, send_ref, kern_ref):
    width = rows_ref.shape[1]
    mine = chosen(own_ref, width)
    x_ref[...] = jnp.dot(rows_ref[...], mine, preferred_element_type=F32).astype(BF16)
    theirs = chosen(other_ref, width)
    send_ref[0:TOK] = jnp.dot(rows_ref[...], theirs, preferred_element_type=F32).astype(BF16)
    send_ref[TOK:] = jnp.zeros((16, send_ref.shape[1]), BF16)
    place = jnp.broadcast_to(place_ref[...].astype(F32), (16, TOK)).astype(BF16)
    send_ref[TOK:, 0:TOK] = place
    kern_ref[...] = jnp.dot(
        kernel_ref[...],
        chosen(own_ref, width, F32),
        precision=lax.Precision.HIGHEST,
        preferred_element_type=F32,
    )


def put_cells(cell_ref, rows, out_ref, first_ref, last_ref):
    count = out_ref.shape[0]
    hit = lax.broadcasted_iota(jnp.int32, (count, count), 0) == cell_ref[...]
    cells = jnp.dot(one_hot(hit), rows, preferred_element_type=F32).astype(BF16)
    out_ref[...] = cells
    first_ref[...] = cells[0:LAYER]
    last_ref[...] = cells[count - LAYER :]


def join_kernel(cell_ref, own_ref, other_ref, *outs):
    put_cells(cell_ref, jnp.concatenate([own_ref[...], other_ref[0:TOK, :]], axis=0), *outs)


def cells_kernel(cell_ref, rows_ref, *outs):
    put_cells(cell_ref, rows_ref[:, rows_ref.shape[1] - outs[0].shape[1] :], *outs)


def in_vmem(body, out_shape, *operands, vmem=None, scalars=0):
    return pl.pallas_call(
        body,
        out_shape=out_shape,
        in_specs=[SMEM] * scalars + [VMEM] * (len(operands) - scalars),
        out_specs=jax.tree.map(lambda _: VMEM, out_shape),
        compiler_params=params(vmem),
    )(*operands)


def fill(before_ref, cells_ref, after_ref, field):
    parts = (before_ref[...], cells_ref[...], after_ref[...])
    lanes = cells_ref.shape[1]
    wide = jnp.concatenate([p.astype(F32) for p in parts], axis=0)
    wide = wide.reshape(6 * 8, 8, lanes)
    column = lax.broadcasted_iota(jnp.int32, wide.shape, 1)
    lower = jnp.where(column == 0, 0.0, jnp.roll(wide, 1, axis=1))
    upper = jnp.where(column == 7, 0.0, jnp.roll(wide, -1, axis=1))
    zero = jnp.zeros((6, 1, 8, lanes), F32)
    for s, value in enumerate((lower, wide, upper)):
        field[s, :, 0:1] = zero
        field[s, :, 9:10] = zero
        field[s, :, 1:9] = value.reshape(6, 8, 8, lanes)


def conv_body(flip, index_ref, kernel_ref, before_ref, cells_ref, after_ref, out_ref, field):
    fill(before_ref, cells_ref, after_ref, field)
    count, lanes = cells_ref.shape
    layers = []
    for z in range(4):
        total = jnp.zeros((8, 8, lanes), F32)
        for o in range(27):
            dz, di, dc = o // 9, o // 3 % 3, o % 3
            row = 26 - o if flip else o
            total = total + kernel_ref[row : row + 1, :][None] * field[dc, z + dz, di : di + 8]
        layers.append(total)
    conv = jnp.stack(layers).reshape(count, lanes)
    result = (cells_ref[...].astype(F32) + conv).astype(BF16)
    hit = lax.broadcasted_iota(jnp.int32, (count, count), 1) == index_ref[...]
    out_ref[...] = jnp.dot(one_hot(hit), result, preferred_element_type=F32).astype(BF16)


def high_part(value):
    return value.astype(BF16)


def rest_part(value):
    return (value - value.astype(BF16).astype(F32)).astype(BF16)


def back_conv_body(index_ref, kernel_ref, before_ref, cells_ref, after_ref, sums_ref, out_ref, field):
    step = pl.program_id(0)
    last = pl.num_programs(0) - 2

    @pl.when(step < last)
    def _():
        conv_body(True, index_ref, kernel_ref, before_ref, cells_ref, after_ref, out_ref, field)

    @pl.when(step == last)
    def _():
        out_ref[...] = high_part(sums_ref[...])

    @pl.when(step == last + 1)
    def _():
        out_ref[...] = rest_part(sums_ref[...])


def tall(rows, steps, lanes=128):
    return pl.BlockSpec((rows, lanes), lambda t: (0, jnp.minimum(t, steps - 1)))


def conv_rows(cells, before, after, kernel, cell_column, sums=None):
    count, width = cells.shape
    steps = width // 128
    specs = [
        pl.BlockSpec((count, 1), lambda t: (0, 0)),
        tall(kernel.shape[0], steps),
        tall(LAYER, steps),
        tall(count, steps),
        tall(LAYER, steps),
    ]
    operands = (cell_column, kernel, before, cells, after)
    if sums is not None:
        specs.append(pl.BlockSpec(sums.shape, lambda t: (0, 0)))
        operands += (sums,)
    wide = steps if sums is None else steps + 2
    return pl.pallas_call(
        functools.partial(conv_body, False) if sums is None else back_conv_body,
        out_shape=jax.ShapeDtypeStruct((count, wide * 128), BF16),
        grid=(wide,),
        in_specs=specs,
        out_specs=pl.BlockSpec((count, 128), lambda t: (0, t)),
        scratch_shapes=[pltpu.VMEM((3, 6, 10, 8, 128), F32)],
    )(*operands)


def grad_body(steps, grad_ref, before_ref, cells_ref, after_ref, out_ref, field):
    @pl.when(pl.program_id(0) >= steps)
    def _():
        out_ref[...] = jnp.zeros_like(out_ref)

    @pl.when(pl.program_id(0) < steps)
    def _():
        fill(before_ref, cells_ref, after_ref, field)
        lanes = cells_ref.shape[1]
        grad = grad_ref[...].astype(F32).reshape(4, 8, 8, lanes)
        sums = []
        for o in range(27):
            dz, di, dc = o // 9, o // 3 % 3, o % 3
            part = grad * field[dc, dz : dz + 4, di : di + 8]
            sums.append(jnp.sum(part.reshape(32, 8, lanes), axis=0))
        sums += [jnp.zeros((8, lanes), F32)] * 5
        out_ref[...] = jnp.sum(jnp.stack(sums), axis=1)


def kernel_grad(grad, cells, before, after):
    count, width = cells.shape
    steps = width // 128
    return pl.pallas_call(
        functools.partial(grad_body, steps),
        out_shape=jax.ShapeDtypeStruct((count, 128), F32),
        grid=(count // 32,),
        in_specs=[tall(count, steps), tall(LAYER, steps), tall(count, steps), tall(LAYER, steps)],
        out_specs=pl.BlockSpec((32, 128), lambda t: (t, 0)),
        scratch_shapes=[pltpu.VMEM((3, 6, 10, 8, 128), F32)],
    )(grad, before, cells, after)


def in_three(value):
    high = value.astype(BF16)
    rest = value - high.astype(F32)
    middle = rest.astype(BF16)
    low = (rest - middle.astype(F32)).astype(BF16)
    return jnp.concatenate([high, middle, low], axis=0)


def pack_rows(block, landed_ref, tiles_ref):
    steps = NY * ROWS // 128
    rows = pick_rows(landed_row(block), TOK, landed_ref[:, 0 : NY * ROWS])
    tiles = [tiles_ref[4 * t : 4 * t + 4].reshape(32, 128) for t in range(steps)]
    return jnp.concatenate([rows, in_three(jnp.concatenate(tiles, axis=1))], axis=0)


def pack_kernel(where_ref, landed_ref, tiles_ref, out_ref):
    out_ref[...] = pack_rows(1 - where_ref[1], landed_ref, tiles_ref)


def last_kernel(where_ref, own_ch, other_ch, landed_ref, tiles_ref, other_ref, out_ref, grad_ref):
    width = out_ref.shape[1]
    contract = (((1,), (1,)), ((), ()))
    own = pack_rows(where_ref[1], landed_ref, tiles_ref)
    total = lax.dot_general(own, chosen(own_ch, width), contract, preferred_element_type=F32)
    total = total + lax.dot_general(
        other_ref[...], chosen(other_ch, width), contract, preferred_element_type=F32
    )
    out_ref[...] = total[0:TOK].astype(BF16)
    grad = total[TOK : TOK + 32] + total[TOK + 32 : TOK + 64] + total[TOK + 64 : TOK + 96]
    grad_ref[...] = grad[0 : grad_ref.shape[0]]


def landed_sum_kernel(landed_ref, out_ref):
    at = NY * ROWS
    parts = landed_ref[:, at : at + 128].astype(F32) + landed_ref[:, at + 128 : at + 256].astype(F32)
    total = jnp.sum(parts.reshape(CHIPS, 8, 128), axis=0)
    for i in range(out_ref.shape[0]):
        out_ref[i] = total


def sum_kernel(count, parts_ref, out_ref):
    total = parts_ref[0]
    for i in range(1, parts_ref.shape[0]):
        total = total + parts_ref[i]
    for i in range(count):
        out_ref[i] = total


def sum_spread(parts, axis, size):
    shape = jax.ShapeDtypeStruct((size, *parts.shape[1:]), F32)
    sent = in_vmem(functools.partial(sum_kernel, size), shape, parts)
    return lax.all_to_all(sent, axis, 0, 0, tiled=True)


def exchange(rows):
    count, width = rows.shape
    sent = rows.reshape(CHIPS, count // CHIPS, width)
    return lax.all_to_all(sent, ("y", "x"), 0, 0, tiled=True).reshape(count, width)


def faces(first, last):
    up = [(i, i + 1) for i in range(CHIPS - 1)]
    down = [(j, i) for i, j in up]
    return lax.ppermute(last, ("y", "x"), up), lax.ppermute(first, ("y", "x"), down)


def shards(planes, tokens, place, kernel, proj_weight, d_projected):
    core = lax.axis_index("c")
    where = jnp.stack([lax.axis_index("y"), core]).astype(jnp.int32)
    rows_x, rows_d = tokens[0], d_projected[0]
    width = rows_x.shape[1]
    local = width // NC

    other_d = swap(rows_d)
    block = after(spread(proj_weight, "x", NX), other_d).reshape(ROWS, proj_weight.shape[1])
    landed_x = exchange(after(rows_x, block))
    near = ring(block, block)
    second_near = ring(*near)

    steps = jnp.arange(local, dtype=jnp.int32)
    first = (steps // GROUP * (NC * GROUP) + steps % GROUP)[None]
    second = first + GROUP
    own_ch = jnp.where(core == 0, first, second)
    other_ch = jnp.where(core == 0, second, first)
    own_x, send_x, kern = in_vmem(
        select_kernel,
        (
            jax.ShapeDtypeStruct((TOK, local), BF16),
            jax.ShapeDtypeStruct((TOK + 16, local), BF16),
            jax.ShapeDtypeStruct((kernel.shape[0], local), F32),
        ),
        own_ch,
        other_ch,
        after(landed_x, *near),
        place,
        kernel,
        vmem=16 << 20,
    )
    other_x = swap(send_x)

    theirs = other_x[TOK, 0:TOK].astype(jnp.int32)
    places = jnp.stack([jnp.where(core == 0, place[0], theirs), jnp.where(core == 0, theirs, place[0])])
    cell = places.reshape(2, CHIPS, 2, 2) + jnp.array([0, TOK], jnp.int32)[:, None, None, None]
    by_block = cell.transpose(2, 1, 0, 3).reshape(2, TOK)
    stacked = jnp.where(core == 0, by_block, by_block[::-1]).reshape(1, 2 * TOK)
    cell = cell.transpose(1, 2, 0, 3).reshape(2 * TOK)
    cell_row, cell_column = cell[None, :], cell[:, None]

    layer = jax.ShapeDtypeStruct((LAYER, local), BF16)
    pair = (jax.ShapeDtypeStruct((2 * TOK, local), BF16), layer, layer)
    third_near = ring(*lax.optimization_barrier((*second_near, own_x))[:2])
    cells_x, first_x, last_x = in_vmem(join_kernel, pair, stacked, own_x, other_x)
    before_x, after_x = faces(first_x, last_x)
    up, down, before_x, after_x = lax.optimization_barrier((*third_near, before_x, after_x))
    far = (shift(up[:CUT], "y", NY, 1), shift(down[CUT:], "y", NY, -1))
    rows_y = conv_rows(cells_x, before_x, after_x, kern, cell_column)

    arrays = (block, *near, *second_near, *third_near, *far)
    sent, whole = back_rows(where, rows_y, rows_d, other_d, arrays)
    landed = exchange(sent)
    cells_d, first_d, last_d = in_vmem(cells_kernel, pair, cell_row, landed)
    before_d, after_d = faces(first_d, last_d)
    sums = kernel_grad(cells_d, cells_x, before_x, after_x)
    back = conv_rows(cells_d, before_d, after_d, kern, cell_column, sums)
    landed = after(landed, back)
    keep, send = project(where, landed, whole)
    landed_d = exchange(back)
    tile = jax.ShapeDtypeStruct((planes, 8, 128), F32)
    tiles = lax.all_to_all(in_vmem(landed_sum_kernel, tile, landed_d), "z", 0, 0, tiled=True)
    tiles = sum_spread(tiles, ("y", "x"), CHIPS)
    packed = jax.ShapeDtypeStruct((TOK + 96, local), BF16)
    d_other = swap(in_vmem(pack_kernel, packed, where, landed_d, tiles, scalars=1))

    projected = (keep + swap(after(send, landed_d))).astype(BF16)
    projected, d_other = lax.optimization_barrier((projected, d_other))
    d_tokens, d_kernel = in_vmem(
        last_kernel,
        (
            jax.ShapeDtypeStruct((TOK, width), BF16),
            jax.ShapeDtypeStruct(kernel.shape, F32),
        ),
        where,
        own_ch,
        other_ch,
        landed_d,
        tiles,
        d_other,
        vmem=16 << 20,
        scalars=1,
    )
    return projected[None], d_tokens[None], d_kernel


def solution(mesh):
    planes = mesh.shape["dp"]
    devices = np.asarray(mesh.devices).reshape(planes, NY, NX, NC)
    grid = Mesh(devices, ("z", "y", "x", "c"))
    seq = ("y", "x", "c")
    return jax.shard_map(
        functools.partial(shards, planes),
        mesh=grid,
        in_specs=(P("z", seq, None), P(seq, None), P(), P(seq, None), P("z", seq, None)),
        out_specs=(P("z", seq, None), P("z", seq, None), P()),
        check_vma=False,
    )
```

```python
import functools

import jax
import jax.numpy as jnp
import numpy as np
from jax import lax
from jax.experimental import pallas as pl
from jax.experimental.pallas import tpu as pltpu
from jax.sharding import Mesh
from jax.sharding import PartitionSpec as P

NY, NX, NC = 8, 4, 2
CHIPS = NY * NX
TOK = 128
LAYER = 64
GROUP = 20
BF16, F32 = jnp.bfloat16, jnp.float32
VMEM = pl.BlockSpec(memory_space=pltpu.VMEM)
SMEM = pl.BlockSpec(memory_space=pltpu.SMEM)
AWAY = pl.BlockSpec(memory_space=pltpu.HBM)


def swap(value):
    return lax.ppermute(value, "c", [(0, 1), (1, 0)])


def spread(value, axis, size):
    return lax.all_to_all(
        jnp.broadcast_to(value[None], (size, *value.shape)), axis, 0, 0, tiled=True
    )


def shift(value, axis, size, step):
    return lax.ppermute(value, axis, [(i, (i + step) % size) for i in range(size)])


def after(value, *others):
    return lax.optimization_barrier((value, *others))[0]


def params(vmem=None):
    return pltpu.CompilerParams(vmem_limit_bytes=vmem)


ROWS = NX * GROUP
CUT = 48
PIECES = [(s, 0, ROWS) for s in (0, -1, 1, -2, 2, -3, 3)] + [(4, 0, CUT), (4, CUT, ROWS - CUT)]


def ring(up, down):
    return shift(up, "y", NY, 1), shift(down, "y", NY, -1)


def assemble(where_ref, arrays, weight, sems, more):
    copies = [
        pltpu.make_async_copy(source, target, sems.at[len(PIECES) + i])
        for i, (source, target) in enumerate(more)
    ]
    for i, (step, skip, rows) in enumerate(PIECES):
        row = pl.multiple_of(lax.rem(where_ref[0] + step + NY, NY) * ROWS + skip, 16)
        copies.append(
            pltpu.make_async_copy(arrays[i], weight.at[pl.ds(row, rows)], sems.at[i])
        )
    for copy in copies:
        copy.start()
    for copy in copies:
        copy.wait()


def one_hot(hit):
    return jnp.where(hit, 1.0, 0.0).astype(BF16)


def pick_rows(source, count, value):
    shape = (count, value.shape[0])
    hit = lax.broadcasted_iota(jnp.int32, shape, 1) == source(
        lax.broadcasted_iota(jnp.int32, shape, 0)
    )
    return jnp.dot(one_hot(hit), value, preferred_element_type=F32).astype(BF16)


def stacked_row(core):
    def source(row):
        block = lax.shift_right_logical(row, 2) & 1
        at = lax.shift_left(lax.shift_right_logical(row, 3), 2) + (row & 3)
        return at + jnp.where(block == core, 0, TOK)

    return source


def landed_row(block):
    def source(row):
        return lax.shift_left(lax.shift_right_logical(row, 2), 3) + (row & 3) + block * 4

    return source


def both_rows(core):
    def source(row):
        block = jnp.where(row < TOK, core, 1 - core)
        return landed_row(block)(row & (TOK - 1))

    return source


def back_kernel(where_ref, y_ref, own_ref, other_ref, *refs):
    arrays, (out_ref, whole_ref, weight, sems, rows) = refs[: len(PIECES)], refs[len(PIECES) :]
    more = [(own_ref, rows.at[0:TOK]), (other_ref, rows.at[TOK:])]
    assemble(where_ref, arrays, weight, sems, more)
    whole = pltpu.make_async_copy(weight, whole_ref, sems.at[len(PIECES) + 2])
    whole.start()
    width = y_ref.shape[1]
    out_ref[:, 0:width] = y_ref[...]
    for at, size in ((0, 256), (256, 256), (512, 128)):
        part = lax.dot_general(
            rows[...],
            weight[at : at + size, :],
            (((1,), (1,)), ((), ())),
            preferred_element_type=F32,
        ).astype(BF16)
        out_ref[:, width + at : width + at + size] = pick_rows(
            stacked_row(where_ref[1]), part.shape[0], part
        )
    whole.wait()


def back_rows(where, rows_y, own, other, arrays):
    columns = own.shape[1]
    return pl.pallas_call(
        back_kernel,
        out_shape=(
            jax.ShapeDtypeStruct((2 * TOK, 2 * NY * ROWS), BF16),
            jax.ShapeDtypeStruct((NY * ROWS, columns), BF16),
        ),
        in_specs=[SMEM, VMEM] + [AWAY] * (2 + len(arrays)),
        out_specs=(VMEM, AWAY),
        scratch_shapes=[
            pltpu.VMEM((NY * ROWS, columns), BF16),
            pltpu.SemaphoreType.DMA((len(PIECES) + 3,)),
            pltpu.VMEM((2 * TOK, columns), BF16),
        ],
        compiler_params=params(60 << 20),
    )(where, rows_y, own, other, *arrays)


def project_kernel(where_ref, landed_ref, whole_ref, keep_ref, send_ref, weight, sem):
    copy = pltpu.make_async_copy(whole_ref, weight, sem)
    copy.start()
    landed = landed_ref[:, 0 : weight.shape[0]]
    rows = pick_rows(both_rows(where_ref[1]), landed.shape[0], landed)
    copy.wait()
    for at in range(0, weight.shape[1], 768):
        part = jnp.dot(rows, weight[:, at : at + 768], preferred_element_type=F32)
        keep_ref[:, at : at + 768] = part[0:TOK]
        send_ref[:, at : at + 768] = part[TOK:]


def project(where, landed, whole):
    out = jax.ShapeDtypeStruct((TOK, whole.shape[1]), F32)
    return pl.pallas_call(
        project_kernel,
        out_shape=(out, out),
        in_specs=[SMEM, VMEM, AWAY],
        out_specs=(VMEM, VMEM),
        scratch_shapes=[pltpu.VMEM(whole.shape, BF16), pltpu.SemaphoreType.DMA],
        compiler_params=params(60 << 20),
        cost_estimate=pl.CostEstimate(
            flops=4 * TOK * whole.size, bytes_accessed=20_000_000, transcendentals=0
        ),
    )(where, landed, whole)


def chosen(channel_ref, width, dtype=BF16):
    shape = (width, channel_ref.shape[1])
    hit = lax.broadcasted_iota(jnp.int32, shape, 0) == channel_ref[...]
    return jnp.where(hit, 1.0, 0.0).astype(dtype)


def select_kernel(own_ref, other_ref, rows_ref, place_ref, kernel_ref, x_ref, send_ref, kern_ref):
    width = rows_ref.shape[1]
    mine = chosen(own_ref, width)
    x_ref[...] = jnp.dot(rows_ref[...], mine, preferred_element_type=F32).astype(BF16)
    theirs = chosen(other_ref, width)
    send_ref[0:TOK] = jnp.dot(rows_ref[...], theirs, preferred_element_type=F32).astype(BF16)
    send_ref[TOK:] = jnp.zeros((16, send_ref.shape[1]), BF16)
    place = jnp.broadcast_to(place_ref[...].astype(F32), (16, TOK)).astype(BF16)
    send_ref[TOK:, 0:TOK] = place
    kern_ref[...] = jnp.dot(
        kernel_ref[...],
        chosen(own_ref, width, F32),
        precision=lax.Precision.HIGHEST,
        preferred_element_type=F32,
    )


def put_cells(cell_ref, rows, out_ref, first_ref, last_ref):
    count = out_ref.shape[0]
    hit = lax.broadcasted_iota(jnp.int32, (count, count), 0) == cell_ref[...]
    cells = jnp.dot(one_hot(hit), rows, preferred_element_type=F32).astype(BF16)
    out_ref[...] = cells
    first_ref[...] = cells[0:LAYER]
    last_ref[...] = cells[count - LAYER :]


def join_kernel(cell_ref, own_ref, other_ref, *outs):
    put_cells(cell_ref, jnp.concatenate([own_ref[...], other_ref[0:TOK, :]], axis=0), *outs)


def cells_kernel(cell_ref, rows_ref, *outs):
    put_cells(cell_ref, rows_ref[:, rows_ref.shape[1] - outs[0].shape[1] :], *outs)


def in_vmem(body, out_shape, *operands, vmem=None, scalars=0):
    return pl.pallas_call(
        body,
        out_shape=out_shape,
        in_specs=[SMEM] * scalars + [VMEM] * (len(operands) - scalars),
        out_specs=jax.tree.map(lambda _: VMEM, out_shape),
        compiler_params=params(vmem),
    )(*operands)


def fill(before_ref, cells_ref, after_ref, field):
    parts = (before_ref[...], cells_ref[...], after_ref[...])
    lanes = cells_ref.shape[1]
    wide = jnp.concatenate([p.astype(F32) for p in parts], axis=0)
    wide = wide.reshape(6 * 8, 8, lanes)
    column = lax.broadcasted_iota(jnp.int32, wide.shape, 1)
    lower = jnp.where(column == 0, 0.0, jnp.roll(wide, 1, axis=1))
    upper = jnp.where(column == 7, 0.0, jnp.roll(wide, -1, axis=1))
    zero = jnp.zeros((6, 1, 8, lanes), F32)
    for s, value in enumerate((lower, wide, upper)):
        field[s, :, 0:1] = zero
        field[s, :, 9:10] = zero
        field[s, :, 1:9] = value.reshape(6, 8, 8, lanes)


def conv_body(flip, index_ref, kernel_ref, before_ref, cells_ref, after_ref, out_ref, field):
    fill(before_ref, cells_ref, after_ref, field)
    count, lanes = cells_ref.shape
    layers = []
    for z in range(4):
        total = jnp.zeros((8, 8, lanes), F32)
        for o in range(27):
            dz, di, dc = o // 9, o // 3 % 3, o % 3
            row = 26 - o if flip else o
            total = total + kernel_ref[row : row + 1, :][None] * field[dc, z + dz, di : di + 8]
        layers.append(total)
    conv = jnp.stack(layers).reshape(count, lanes)
    result = (cells_ref[...].astype(F32) + conv).astype(BF16)
    hit = lax.broadcasted_iota(jnp.int32, (count, count), 1) == index_ref[...]
    out_ref[...] = jnp.dot(one_hot(hit), result, preferred_element_type=F32).astype(BF16)


def high_part(value):
    return value.astype(BF16)


def rest_part(value):
    return (value - value.astype(BF16).astype(F32)).astype(BF16)


def back_conv_body(index_ref, kernel_ref, before_ref, cells_ref, after_ref, sums_ref, out_ref, field):
    step = pl.program_id(0)
    last = pl.num_programs(0) - 2

    @pl.when(step < last)
    def _():
        conv_body(True, index_ref, kernel_ref, before_ref, cells_ref, after_ref, out_ref, field)

    @pl.when(step == last)
    def _():
        out_ref[...] = high_part(sums_ref[...])

    @pl.when(step == last + 1)
    def _():
        out_ref[...] = rest_part(sums_ref[...])


def tall(rows, steps, lanes=128):
    return pl.BlockSpec((rows, lanes), lambda t: (0, jnp.minimum(t, steps - 1)))


def conv_rows(cells, before, after, kernel, cell_column, sums=None):
    count, width = cells.shape
    steps = width // 128
    specs = [
        pl.BlockSpec((count, 1), lambda t: (0, 0)),
        tall(kernel.shape[0], steps),
        tall(LAYER, steps),
        tall(count, steps),
        tall(LAYER, steps),
    ]
    operands = (cell_column, kernel, before, cells, after)
    if sums is not None:
        specs.append(pl.BlockSpec(sums.shape, lambda t: (0, 0)))
        operands += (sums,)
    wide = steps if sums is None else steps + 2
    return pl.pallas_call(
        functools.partial(conv_body, False) if sums is None else back_conv_body,
        out_shape=jax.ShapeDtypeStruct((count, wide * 128), BF16),
        grid=(wide,),
        in_specs=specs,
        out_specs=pl.BlockSpec((count, 128), lambda t: (0, t)),
        scratch_shapes=[pltpu.VMEM((3, 6, 10, 8, 128), F32)],
    )(*operands)


def grad_body(steps, grad_ref, before_ref, cells_ref, after_ref, out_ref, field):
    @pl.when(pl.program_id(0) >= steps)
    def _():
        out_ref[...] = jnp.zeros_like(out_ref)

    @pl.when(pl.program_id(0) < steps)
    def _():
        fill(before_ref, cells_ref, after_ref, field)
        lanes = cells_ref.shape[1]
        grad = grad_ref[...].astype(F32).reshape(4, 8, 8, lanes)
        sums = []
        for o in range(27):
            dz, di, dc = o // 9, o // 3 % 3, o % 3
            part = grad * field[dc, dz : dz + 4, di : di + 8]
            sums.append(jnp.sum(part.reshape(32, 8, lanes), axis=0))
        sums += [jnp.zeros((8, lanes), F32)] * 5
        out_ref[...] = jnp.sum(jnp.stack(sums), axis=1)


def kernel_grad(grad, cells, before, after):
    count, width = cells.shape
    steps = width // 128
    return pl.pallas_call(
        functools.partial(grad_body, steps),
        out_shape=jax.ShapeDtypeStruct((count, 128), F32),
        grid=(count // 32,),
        in_specs=[tall(count, steps), tall(LAYER, steps), tall(count, steps), tall(LAYER, steps)],
        out_specs=pl.BlockSpec((32, 128), lambda t: (t, 0)),
        scratch_shapes=[pltpu.VMEM((3, 6, 10, 8, 128), F32)],
    )(grad, before, cells, after)


def in_three(value):
    high = value.astype(BF16)
    rest = value - high.astype(F32)
    middle = rest.astype(BF16)
    low = (rest - middle.astype(F32)).astype(BF16)
    return jnp.concatenate([high, middle, low], axis=0)


def pack_rows(block, landed_ref, tiles_ref):
    steps = NY * ROWS // 128
    rows = pick_rows(landed_row(block), TOK, landed_ref[:, 0 : NY * ROWS])
    tiles = [tiles_ref[4 * t : 4 * t + 4].reshape(32, 128) for t in range(steps)]
    return jnp.concatenate([rows, in_three(jnp.concatenate(tiles, axis=1))], axis=0)


def pack_kernel(where_ref, landed_ref, tiles_ref, out_ref):
    out_ref[...] = pack_rows(1 - where_ref[1], landed_ref, tiles_ref)


def last_kernel(where_ref, own_ch, other_ch, landed_ref, tiles_ref, other_ref, out_ref, grad_ref):
    width = out_ref.shape[1]
    contract = (((1,), (1,)), ((), ()))
    own = pack_rows(where_ref[1], landed_ref, tiles_ref)
    total = lax.dot_general(own, chosen(own_ch, width), contract, preferred_element_type=F32)
    total = total + lax.dot_general(
        other_ref[...], chosen(other_ch, width), contract, preferred_element_type=F32
    )
    out_ref[...] = total[0:TOK].astype(BF16)
    grad = total[TOK : TOK + 32] + total[TOK + 32 : TOK + 64] + total[TOK + 64 : TOK + 96]
    grad_ref[...] = grad[0 : grad_ref.shape[0]]


def landed_sum_kernel(landed_ref, out_ref):
    at = NY * ROWS
    parts = landed_ref[:, at : at + 128].astype(F32) + landed_ref[:, at + 128 : at + 256].astype(F32)
    total = jnp.sum(parts.reshape(CHIPS, 8, 128), axis=0)
    for i in range(out_ref.shape[0]):
        out_ref[i] = total


def sum_kernel(count, parts_ref, out_ref):
    total = parts_ref[0]
    for i in range(1, parts_ref.shape[0]):
        total = total + parts_ref[i]
    for i in range(count):
        out_ref[i] = total


def sum_spread(parts, axis, size):
    shape = jax.ShapeDtypeStruct((size, *parts.shape[1:]), F32)
    sent = in_vmem(functools.partial(sum_kernel, size), shape, parts)
    return lax.all_to_all(sent, axis, 0, 0, tiled=True)


def exchange(rows):
    count, width = rows.shape
    sent = rows.reshape(CHIPS, count // CHIPS, width)
    return lax.all_to_all(sent, ("y", "x"), 0, 0, tiled=True).reshape(count, width)


def faces(first, last):
    up = [(i, i + 1) for i in range(CHIPS - 1)]
    down = [(j, i) for i, j in up]
    return lax.ppermute(last, ("y", "x"), up), lax.ppermute(first, ("y", "x"), down)


def shards(planes, tokens, place, kernel, proj_weight, d_projected):
    core = lax.axis_index("c")
    where = jnp.stack([lax.axis_index("y"), core]).astype(jnp.int32)
    rows_x, rows_d = tokens[0], d_projected[0]
    width = rows_x.shape[1]
    local = width // NC

    other_d = swap(rows_d)
    block = after(spread(proj_weight, "x", NX), other_d).reshape(ROWS, proj_weight.shape[1])
    landed_x = exchange(after(rows_x, block))
    near = ring(block, block)
    second_near = ring(*near)

    steps = jnp.arange(local, dtype=jnp.int32)
    first = (steps // GROUP * (NC * GROUP) + steps % GROUP)[None]
    second = first + GROUP
    own_ch = jnp.where(core == 0, first, second)
    other_ch = jnp.where(core == 0, second, first)
    own_x, send_x, kern = in_vmem(
        select_kernel,
        (
            jax.ShapeDtypeStruct((TOK, local), BF16),
            jax.ShapeDtypeStruct((TOK + 16, local), BF16),
            jax.ShapeDtypeStruct((kernel.shape[0], local), F32),
        ),
        own_ch,
        other_ch,
        after(landed_x, *near),
        place,
        kernel,
        vmem=16 << 20,
    )
    other_x = swap(send_x)

    theirs = other_x[TOK, 0:TOK].astype(jnp.int32)
    places = jnp.stack([jnp.where(core == 0, place[0], theirs), jnp.where(core == 0, theirs, place[0])])
    cell = places.reshape(2, CHIPS, 2, 2) + jnp.array([0, TOK], jnp.int32)[:, None, None, None]
    by_block = cell.transpose(2, 1, 0, 3).reshape(2, TOK)
    stacked = jnp.where(core == 0, by_block, by_block[::-1]).reshape(1, 2 * TOK)
    cell = cell.transpose(1, 2, 0, 3).reshape(2 * TOK)
    cell_row, cell_column = cell[None, :], cell[:, None]

    layer = jax.ShapeDtypeStruct((LAYER, local), BF16)
    pair = (jax.ShapeDtypeStruct((2 * TOK, local), BF16), layer, layer)
    third_near = ring(*lax.optimization_barrier((*second_near, own_x))[:2])
    cells_x, first_x, last_x = in_vmem(join_kernel, pair, stacked, own_x, other_x)
    before_x, after_x = faces(first_x, last_x)
    up, down, before_x, after_x = lax.optimization_barrier((*third_near, before_x, after_x))
    far = (shift(up[:CUT], "y", NY, 1), shift(down[CUT:], "y", NY, -1))
    rows_y = conv_rows(cells_x, before_x, after_x, kern, cell_column)

    arrays = (block, *near, *second_near, *third_near, *far)
    sent, whole = back_rows(where, rows_y, rows_d, other_d, arrays)
    landed = exchange(sent)
    cells_d, first_d, last_d = in_vmem(cells_kernel, pair, cell_row, landed)
    before_d, after_d = faces(first_d, last_d)
    sums = kernel_grad(cells_d, cells_x, before_x, after_x)
    back = conv_rows(cells_d, before_d, after_d, kern, cell_column, sums)
    landed = after(landed, back)
    keep, send = project(where, landed, whole)
    landed_d = exchange(back)
    tile = jax.ShapeDtypeStruct((planes, 8, 128), F32)
    tiles = lax.all_to_all(in_vmem(landed_sum_kernel, tile, landed_d), "z", 0, 0, tiled=True)
    tiles = sum_spread(tiles, ("y", "x"), CHIPS)
    projected = (keep + swap(after(send, landed_d))).astype(BF16)
    tiles, projected = lax.optimization_barrier((tiles, projected))
    packed = jax.ShapeDtypeStruct((TOK + 96, local), BF16)
    d_other = swap(in_vmem(pack_kernel, packed, where, landed_d, tiles, scalars=1))

    d_tokens, d_kernel = in_vmem(
        last_kernel,
        (
            jax.ShapeDtypeStruct((TOK, width), BF16),
            jax.ShapeDtypeStruct(kernel.shape, F32),
        ),
        where,
        own_ch,
        other_ch,
        landed_d,
        tiles,
        d_other,
        vmem=16 << 20,
        scalars=1,
    )
    return projected[None], d_tokens[None], d_kernel


def solution(mesh):
    planes = mesh.shape["dp"]
    devices = np.asarray(mesh.devices).reshape(planes, NY, NX, NC)
    grid = Mesh(devices, ("z", "y", "x", "c"))
    seq = ("y", "x", "c")
    return jax.shard_map(
        functools.partial(shards, planes),
        mesh=grid,
        in_specs=(P("z", seq, None), P(seq, None), P(), P(seq, None), P("z", seq, None)),
        out_specs=(P("z", seq, None), P("z", seq, None), P()),
        check_vma=False,
    )
```

```python
import functools

import jax
import jax.numpy as jnp
import numpy as np
from jax import lax
from jax.experimental import pallas as pl
from jax.experimental.pallas import tpu as pltpu
from jax.sharding import Mesh
from jax.sharding import PartitionSpec as P

NY, NX, NC = 8, 4, 2
CHIPS = NY * NX
TOK = 128
LAYER = 64
GROUP = 20
BF16, F32 = jnp.bfloat16, jnp.float32
VMEM = pl.BlockSpec(memory_space=pltpu.VMEM)
SMEM = pl.BlockSpec(memory_space=pltpu.SMEM)
AWAY = pl.BlockSpec(memory_space=pltpu.HBM)


def swap(value):
    return lax.ppermute(value, "c", [(0, 1), (1, 0)])


def spread(value, axis, size):
    return lax.all_to_all(
        jnp.broadcast_to(value[None], (size, *value.shape)), axis, 0, 0, tiled=True
    )


def shift(value, axis, size, step):
    return lax.ppermute(value, axis, [(i, (i + step) % size) for i in range(size)])


def after(value, *others):
    return lax.optimization_barrier((value, *others))[0]


def params(vmem=None):
    return pltpu.CompilerParams(vmem_limit_bytes=vmem)


ROWS = NX * GROUP
CUT = 48
PIECES = [(s, 0, ROWS) for s in (0, -1, 1, -2, 2, -3, 3)] + [(4, 0, CUT), (4, CUT, ROWS - CUT)]


def ring(up, down):
    return shift(up, "y", NY, 1), shift(down, "y", NY, -1)


def assemble(where_ref, arrays, weight, sems, more):
    copies = [
        pltpu.make_async_copy(source, target, sems.at[len(PIECES) + i])
        for i, (source, target) in enumerate(more)
    ]
    for i, (step, skip, rows) in enumerate(PIECES):
        row = pl.multiple_of(lax.rem(where_ref[0] + step + NY, NY) * ROWS + skip, 16)
        copies.append(
            pltpu.make_async_copy(arrays[i], weight.at[pl.ds(row, rows)], sems.at[i])
        )
    for copy in copies:
        copy.start()
    for copy in copies:
        copy.wait()


def one_hot(hit):
    return jnp.where(hit, 1.0, 0.0).astype(BF16)


def pick_rows(source, count, value):
    shape = (count, value.shape[0])
    hit = lax.broadcasted_iota(jnp.int32, shape, 1) == source(
        lax.broadcasted_iota(jnp.int32, shape, 0)
    )
    return jnp.dot(one_hot(hit), value, preferred_element_type=F32).astype(BF16)


def stacked_row(core):
    def source(row):
        block = lax.shift_right_logical(row, 2) & 1
        at = lax.shift_left(lax.shift_right_logical(row, 3), 2) + (row & 3)
        return at + jnp.where(block == core, 0, TOK)

    return source


def landed_row(block):
    def source(row):
        return lax.shift_left(lax.shift_right_logical(row, 2), 3) + (row & 3) + block * 4

    return source


def both_rows(core):
    def source(row):
        block = jnp.where(row < TOK, core, 1 - core)
        return landed_row(block)(row & (TOK - 1))

    return source


def back_kernel(where_ref, y_ref, own_ref, other_ref, *refs):
    arrays, (out_ref, whole_ref, weight, sems, rows) = refs[: len(PIECES)], refs[len(PIECES) :]
    more = [(own_ref, rows.at[0:TOK]), (other_ref, rows.at[TOK:])]
    assemble(where_ref, arrays, weight, sems, more)
    whole = pltpu.make_async_copy(weight, whole_ref, sems.at[len(PIECES) + 2])
    whole.start()
    width = y_ref.shape[1]
    out_ref[:, 0:width] = y_ref[...]
    for at, size in ((0, 256), (256, 256), (512, 128)):
        part = lax.dot_general(
            rows[...],
            weight[at : at + size, :],
            (((1,), (1,)), ((), ())),
            preferred_element_type=F32,
        ).astype(BF16)
        out_ref[:, width + at : width + at + size] = pick_rows(
            stacked_row(where_ref[1]), part.shape[0], part
        )
    whole.wait()


def back_rows(where, rows_y, own, other, arrays):
    columns = own.shape[1]
    return pl.pallas_call(
        back_kernel,
        out_shape=(
            jax.ShapeDtypeStruct((2 * TOK, 2 * NY * ROWS), BF16),
            jax.ShapeDtypeStruct((NY * ROWS, columns), BF16),
        ),
        in_specs=[SMEM, VMEM] + [AWAY] * (2 + len(arrays)),
        out_specs=(VMEM, AWAY),
        scratch_shapes=[
            pltpu.VMEM((NY * ROWS, columns), BF16),
            pltpu.SemaphoreType.DMA((len(PIECES) + 3,)),
            pltpu.VMEM((2 * TOK, columns), BF16),
        ],
        compiler_params=params(60 << 20),
    )(where, rows_y, own, other, *arrays)


def project_kernel(where_ref, landed_ref, whole_ref, keep_ref, send_ref, weight, sem):
    copy = pltpu.make_async_copy(whole_ref, weight, sem)
    copy.start()
    landed = landed_ref[:, 0 : weight.shape[0]]
    rows = pick_rows(both_rows(where_ref[1]), landed.shape[0], landed)
    copy.wait()
    for at in range(0, weight.shape[1], 768):
        part = jnp.dot(rows, weight[:, at : at + 768], preferred_element_type=F32)
        keep_ref[:, at : at + 768] = part[0:TOK]
        send_ref[:, at : at + 768] = part[TOK:]


def project(where, landed, whole):
    out = jax.ShapeDtypeStruct((TOK, whole.shape[1]), F32)
    return pl.pallas_call(
        project_kernel,
        out_shape=(out, out),
        in_specs=[SMEM, VMEM, AWAY],
        out_specs=(VMEM, VMEM),
        scratch_shapes=[pltpu.VMEM(whole.shape, BF16), pltpu.SemaphoreType.DMA],
        compiler_params=params(60 << 20),
        cost_estimate=pl.CostEstimate(
            flops=4 * TOK * whole.size, bytes_accessed=20_000_000, transcendentals=0
        ),
    )(where, landed, whole)


def chosen(channel_ref, width, dtype=BF16):
    shape = (width, channel_ref.shape[1])
    hit = lax.broadcasted_iota(jnp.int32, shape, 0) == channel_ref[...]
    return jnp.where(hit, 1.0, 0.0).astype(dtype)


def select_kernel(own_ref, other_ref, rows_ref, place_ref, kernel_ref, x_ref, send_ref, kern_ref):
    width = rows_ref.shape[1]
    mine = chosen(own_ref, width)
    x_ref[...] = jnp.dot(rows_ref[...], mine, preferred_element_type=F32).astype(BF16)
    theirs = chosen(other_ref, width)
    send_ref[0:TOK] = jnp.dot(rows_ref[...], theirs, preferred_element_type=F32).astype(BF16)
    send_ref[TOK:] = jnp.zeros((16, send_ref.shape[1]), BF16)
    place = jnp.broadcast_to(place_ref[...].astype(F32), (16, TOK)).astype(BF16)
    send_ref[TOK:, 0:TOK] = place
    kern_ref[...] = jnp.dot(
        kernel_ref[...],
        chosen(own_ref, width, F32),
        precision=lax.Precision.HIGHEST,
        preferred_element_type=F32,
    )


def put_cells(cell_ref, rows, out_ref, first_ref, last_ref):
    count = out_ref.shape[0]
    hit = lax.broadcasted_iota(jnp.int32, (count, count), 0) == cell_ref[...]
    cells = jnp.dot(one_hot(hit), rows, preferred_element_type=F32).astype(BF16)
    out_ref[...] = cells
    first_ref[...] = cells[0:LAYER]
    last_ref[...] = cells[count - LAYER :]


def join_kernel(cell_ref, own_ref, other_ref, *outs):
    put_cells(cell_ref, jnp.concatenate([own_ref[...], other_ref[0:TOK, :]], axis=0), *outs)


def cells_kernel(cell_ref, rows_ref, *outs):
    put_cells(cell_ref, rows_ref[:, rows_ref.shape[1] - outs[0].shape[1] :], *outs)


def in_vmem(body, out_shape, *operands, vmem=None, scalars=0):
    return pl.pallas_call(
        body,
        out_shape=out_shape,
        in_specs=[SMEM] * scalars + [VMEM] * (len(operands) - scalars),
        out_specs=jax.tree.map(lambda _: VMEM, out_shape),
        compiler_params=params(vmem),
    )(*operands)


def fill(before_ref, cells_ref, after_ref, field):
    lanes = cells_ref.shape[1]
    zero = jnp.zeros((6, 1, 8, lanes), F32)
    field[:, 0:1] = zero
    field[:, 9:10] = zero
    field[0:1, 1:9] = before_ref[...].astype(F32).reshape(1, 8, 8, lanes)
    field[1:5, 1:9] = cells_ref[...].astype(F32).reshape(4, 8, 8, lanes)
    field[5:6, 1:9] = after_ref[...].astype(F32).reshape(1, 8, 8, lanes)


def from_lower(value):
    column = lax.broadcasted_iota(jnp.int32, value.shape, value.ndim - 2)
    return jnp.where(column == 0, 0.0, jnp.roll(value, 1, axis=value.ndim - 2))


def from_upper(value):
    column = lax.broadcasted_iota(jnp.int32, value.shape, value.ndim - 2)
    return jnp.where(column == 7, 0.0, jnp.roll(value, -1, axis=value.ndim - 2))


def conv_body(flip, index_ref, kernel_ref, before_ref, cells_ref, after_ref, out_ref, field):
    fill(before_ref, cells_ref, after_ref, field)
    count, lanes = cells_ref.shape
    layers = []
    for z in range(4):
        sums = []
        for dc in range(3):
            total = None
            for o in range(dc, 27, 3):
                dz, di = o // 9, o // 3 % 3
                row = 26 - o if flip else o
                term = kernel_ref[row : row + 1, :][None] * field[z + dz, di : di + 8]
                total = term if total is None else total + term
            sums.append(total)
        layers.append(sums[1] + from_lower(sums[0]) + from_upper(sums[2]))
    conv = jnp.stack(layers).reshape(count, lanes)
    result = (cells_ref[...].astype(F32) + conv).astype(BF16)
    hit = lax.broadcasted_iota(jnp.int32, (count, count), 1) == index_ref[...]
    out_ref[...] = jnp.dot(one_hot(hit), result, preferred_element_type=F32).astype(BF16)


def high_part(value):
    return value.astype(BF16)


def rest_part(value):
    return (value - value.astype(BF16).astype(F32)).astype(BF16)


def back_conv_body(index_ref, kernel_ref, before_ref, cells_ref, after_ref, sums_ref, out_ref, field):
    step = pl.program_id(0)
    last = pl.num_programs(0) - 2

    @pl.when(step < last)
    def _():
        conv_body(True, index_ref, kernel_ref, before_ref, cells_ref, after_ref, out_ref, field)

    @pl.when(step == last)
    def _():
        out_ref[...] = high_part(sums_ref[...])

    @pl.when(step == last + 1)
    def _():
        out_ref[...] = rest_part(sums_ref[...])


def tall(rows, steps, lanes=128):
    return pl.BlockSpec((rows, lanes), lambda t: (0, jnp.minimum(t, steps - 1)))


def conv_rows(cells, before, after, kernel, cell_column, sums=None):
    count, width = cells.shape
    steps = width // 128
    specs = [
        pl.BlockSpec((count, 1), lambda t: (0, 0)),
        tall(kernel.shape[0], steps),
        tall(LAYER, steps),
        tall(count, steps),
        tall(LAYER, steps),
    ]
    operands = (cell_column, kernel, before, cells, after)
    if sums is not None:
        specs.append(pl.BlockSpec(sums.shape, lambda t: (0, 0)))
        operands += (sums,)
    wide = steps if sums is None else steps + 2
    return pl.pallas_call(
        functools.partial(conv_body, False) if sums is None else back_conv_body,
        out_shape=jax.ShapeDtypeStruct((count, wide * 128), BF16),
        grid=(wide,),
        in_specs=specs,
        out_specs=pl.BlockSpec((count, 128), lambda t: (0, t)),
        scratch_shapes=[pltpu.VMEM((6, 10, 8, 128), F32)],
    )(*operands)


def grad_body(steps, grad_ref, before_ref, cells_ref, after_ref, out_ref, field):
    @pl.when(pl.program_id(0) >= steps)
    def _():
        out_ref[...] = jnp.zeros_like(out_ref)

    @pl.when(pl.program_id(0) < steps)
    def _():
        fill(before_ref, cells_ref, after_ref, field)
        lanes = cells_ref.shape[1]
        grad = grad_ref[...].astype(F32).reshape(4, 8, 8, lanes)
        shifted = (from_upper(grad), grad, from_lower(grad))
        sums = []
        for o in range(27):
            dz, di, dc = o // 9, o // 3 % 3, o % 3
            part = shifted[dc] * field[dz : dz + 4, di : di + 8]
            sums.append(jnp.sum(part.reshape(32, 8, lanes), axis=0))
        sums += [jnp.zeros((8, lanes), F32)] * 5
        out_ref[...] = jnp.sum(jnp.stack(sums), axis=1)


def kernel_grad(grad, cells, before, after):
    count, width = cells.shape
    steps = width // 128
    return pl.pallas_call(
        functools.partial(grad_body, steps),
        out_shape=jax.ShapeDtypeStruct((count, 128), F32),
        grid=(count // 32,),
        in_specs=[tall(count, steps), tall(LAYER, steps), tall(count, steps), tall(LAYER, steps)],
        out_specs=pl.BlockSpec((32, 128), lambda t: (t, 0)),
        scratch_shapes=[pltpu.VMEM((6, 10, 8, 128), F32)],
    )(grad, before, cells, after)


def in_three(value):
    high = value.astype(BF16)
    rest = value - high.astype(F32)
    middle = rest.astype(BF16)
    low = (rest - middle.astype(F32)).astype(BF16)
    return jnp.concatenate([high, middle, low], axis=0)


def stack_parts(rows, tiles_ref):
    steps = NY * ROWS // 128
    tiles = [tiles_ref[4 * t : 4 * t + 4].reshape(32, 128) for t in range(steps)]
    return jnp.concatenate([rows, in_three(jnp.concatenate(tiles, axis=1))], axis=0)


def other_kernel(where_ref, landed_ref, out_ref):
    out_ref[...] = pick_rows(
        landed_row(1 - where_ref[1]), TOK, landed_ref[:, 0 : NY * ROWS]
    )


def last_kernel(where_ref, own_ch, other_ch, landed_ref, tiles_ref, rows_ref, other_ref, out_ref, grad_ref):
    width = out_ref.shape[1]
    contract = (((1,), (1,)), ((), ()))
    rows = pick_rows(landed_row(where_ref[1]), TOK, landed_ref[:, 0 : NY * ROWS])
    own = stack_parts(rows, tiles_ref)
    other = stack_parts(rows_ref[...], other_ref)
    total = lax.dot_general(own, chosen(own_ch, width), contract, preferred_element_type=F32)
    total = total + lax.dot_general(
        other, chosen(other_ch, width), contract, preferred_element_type=F32
    )
    out_ref[...] = total[0:TOK].astype(BF16)
    grad = total[TOK : TOK + 32] + total[TOK + 32 : TOK + 64] + total[TOK + 64 : TOK + 96]
    grad_ref[...] = grad[0 : grad_ref.shape[0]]


def landed_sum_kernel(landed_ref, out_ref):
    at = NY * ROWS
    parts = landed_ref[:, at : at + 128].astype(F32) + landed_ref[:, at + 128 : at + 256].astype(F32)
    total = jnp.sum(parts.reshape(CHIPS, 8, 128), axis=0)
    for i in range(out_ref.shape[0]):
        out_ref[i] = total


def sum_kernel(count, parts_ref, out_ref):
    total = parts_ref[0]
    for i in range(1, parts_ref.shape[0]):
        total = total + parts_ref[i]
    for i in range(count):
        out_ref[i] = total


def sum_spread(parts, axis, size):
    shape = jax.ShapeDtypeStruct((size, *parts.shape[1:]), F32)
    sent = in_vmem(functools.partial(sum_kernel, size), shape, parts)
    return lax.all_to_all(sent, axis, 0, 0, tiled=True)


def exchange(rows):
    count, width = rows.shape
    sent = rows.reshape(CHIPS, count // CHIPS, width)
    return lax.all_to_all(sent, ("y", "x"), 0, 0, tiled=True).reshape(count, width)


def faces(first, last):
    up = [(i, i + 1) for i in range(CHIPS - 1)]
    down = [(j, i) for i, j in up]
    return lax.ppermute(last, ("y", "x"), up), lax.ppermute(first, ("y", "x"), down)


def shards(planes, tokens, place, kernel, proj_weight, d_projected):
    core = lax.axis_index("c")
    where = jnp.stack([lax.axis_index("y"), core]).astype(jnp.int32)
    rows_x, rows_d = tokens[0], d_projected[0]
    width = rows_x.shape[1]
    local = width // NC

    other_d = swap(rows_d)
    block = after(spread(proj_weight, "x", NX), other_d).reshape(ROWS, proj_weight.shape[1])
    landed_x = exchange(after(rows_x, block))
    near = ring(block, block)
    second_near = ring(*near)

    steps = jnp.arange(local, dtype=jnp.int32)
    first = (steps // GROUP * (NC * GROUP) + steps % GROUP)[None]
    second = first + GROUP
    own_ch = jnp.where(core == 0, first, second)
    other_ch = jnp.where(core == 0, second, first)
    own_x, send_x, kern = in_vmem(
        select_kernel,
        (
            jax.ShapeDtypeStruct((TOK, local), BF16),
            jax.ShapeDtypeStruct((TOK + 16, local), BF16),
            jax.ShapeDtypeStruct((kernel.shape[0], local), F32),
        ),
        own_ch,
        other_ch,
        after(landed_x, *near),
        place,
        kernel,
        vmem=16 << 20,
    )
    other_x = swap(send_x)

    theirs = other_x[TOK, 0:TOK].astype(jnp.int32)
    places = jnp.stack([jnp.where(core == 0, place[0], theirs), jnp.where(core == 0, theirs, place[0])])
    cell = places.reshape(2, CHIPS, 2, 2) + jnp.array([0, TOK], jnp.int32)[:, None, None, None]
    by_block = cell.transpose(2, 1, 0, 3).reshape(2, TOK)
    stacked = jnp.where(core == 0, by_block, by_block[::-1]).reshape(1, 2 * TOK)
    cell = cell.transpose(1, 2, 0, 3).reshape(2 * TOK)
    cell_row, cell_column = cell[None, :], cell[:, None]

    layer = jax.ShapeDtypeStruct((LAYER, local), BF16)
    pair = (jax.ShapeDtypeStruct((2 * TOK, local), BF16), layer, layer)
    third_near = ring(*lax.optimization_barrier((*second_near, own_x))[:2])
    cells_x, first_x, last_x = in_vmem(join_kernel, pair, stacked, own_x, other_x)
    before_x, after_x = faces(first_x, last_x)
    up, down, before_x, after_x = lax.optimization_barrier((*third_near, before_x, after_x))
    far = (shift(up[:CUT], "y", NY, 1), shift(down[CUT:], "y", NY, -1))
    rows_y = conv_rows(cells_x, before_x, after_x, kern, cell_column)

    arrays = (block, *near, *second_near, *third_near, *far)
    sent, whole = back_rows(where, rows_y, rows_d, other_d, arrays)
    landed = exchange(sent)
    cells_d, first_d, last_d = in_vmem(cells_kernel, pair, cell_row, landed)
    before_d, after_d = faces(first_d, last_d)
    sums = kernel_grad(cells_d, cells_x, before_x, after_x)
    back = conv_rows(cells_d, before_d, after_d, kern, cell_column, sums)
    landed = after(landed, back)
    keep, send = project(where, landed, whole)
    landed_d = exchange(back)
    tile = jax.ShapeDtypeStruct((planes, 8, 128), F32)
    tiles = lax.all_to_all(in_vmem(landed_sum_kernel, tile, landed_d), "z", 0, 0, tiled=True)
    other_rows = jax.ShapeDtypeStruct((TOK, local), BF16)
    d_other = swap(in_vmem(other_kernel, other_rows, where, landed_d, scalars=1))
    tiles = sum_spread(after(tiles, d_other), ("y", "x"), CHIPS)
    projected = (keep + swap(after(send, landed_d))).astype(BF16)
    tiles, projected = lax.optimization_barrier((tiles, projected))

    d_tokens, d_kernel = in_vmem(
        last_kernel,
        (
            jax.ShapeDtypeStruct((TOK, width), BF16),
            jax.ShapeDtypeStruct(kernel.shape, F32),
        ),
        where,
        own_ch,
        other_ch,
        landed_d,
        tiles,
        d_other,
        swap(tiles),
        vmem=16 << 20,
        scalars=1,
    )
    return projected[None], d_tokens[None], d_kernel


def solution(mesh):
    planes = mesh.shape["dp"]
    devices = np.asarray(mesh.devices).reshape(planes, NY, NX, NC)
    grid = Mesh(devices, ("z", "y", "x", "c"))
    seq = ("y", "x", "c")
    return jax.shard_map(
        functools.partial(shards, planes),
        mesh=grid,
        in_specs=(P("z", seq, None), P(seq, None), P(), P(seq, None), P("z", seq, None)),
        out_specs=(P("z", seq, None), P("z", seq, None), P()),
        check_vma=False,
    )
```

```python
import functools

import jax
import jax.numpy as jnp
import numpy as np
from jax import lax
from jax.experimental import pallas as pl
from jax.experimental.pallas import tpu as pltpu
from jax.sharding import Mesh
from jax.sharding import PartitionSpec as P

NY, NX, NC = 8, 4, 2
CHIPS = NY * NX
TOK = 128
LAYER = 64
GROUP = 20
BF16, F32 = jnp.bfloat16, jnp.float32
VMEM = pl.BlockSpec(memory_space=pltpu.VMEM)
SMEM = pl.BlockSpec(memory_space=pltpu.SMEM)
AWAY = pl.BlockSpec(memory_space=pltpu.HBM)


def swap(value):
    return lax.ppermute(value, "c", [(0, 1), (1, 0)])


def spread(value, axis, size):
    return lax.all_to_all(
        jnp.broadcast_to(value[None], (size, *value.shape)), axis, 0, 0, tiled=True
    )


def shift(value, axis, size, step):
    return lax.ppermute(value, axis, [(i, (i + step) % size) for i in range(size)])


def after(value, *others):
    return lax.optimization_barrier((value, *others))[0]


def params(vmem=None):
    return pltpu.CompilerParams(vmem_limit_bytes=vmem)


ROWS = NX * GROUP
CUT = 48
PIECES = [(s, 0, ROWS) for s in (0, -1, 1, -2, 2, -3, 3)] + [(4, 0, CUT), (4, CUT, ROWS - CUT)]


def ring(up, down):
    return shift(up, "y", NY, 1), shift(down, "y", NY, -1)


def assemble(where_ref, arrays, weight, sems, more):
    copies = [
        pltpu.make_async_copy(source, target, sems.at[len(PIECES) + i])
        for i, (source, target) in enumerate(more)
    ]
    for i, (step, skip, rows) in enumerate(PIECES):
        row = pl.multiple_of(lax.rem(where_ref[0] + step + NY, NY) * ROWS + skip, 16)
        copies.append(
            pltpu.make_async_copy(arrays[i], weight.at[pl.ds(row, rows)], sems.at[i])
        )
    for copy in copies:
        copy.start()
    for copy in copies:
        copy.wait()


def one_hot(hit):
    return jnp.where(hit, 1.0, 0.0).astype(BF16)


def pick_rows(source, count, value):
    shape = (count, value.shape[0])
    hit = lax.broadcasted_iota(jnp.int32, shape, 1) == source(
        lax.broadcasted_iota(jnp.int32, shape, 0)
    )
    return jnp.dot(one_hot(hit), value, preferred_element_type=F32).astype(BF16)


def stacked_row(core):
    def source(row):
        block = lax.shift_right_logical(row, 2) & 1
        at = lax.shift_left(lax.shift_right_logical(row, 3), 2) + (row & 3)
        return at + jnp.where(block == core, 0, TOK)

    return source


def landed_row(block):
    def source(row):
        return lax.shift_left(lax.shift_right_logical(row, 2), 3) + (row & 3) + block * 4

    return source


def both_rows(core):
    def source(row):
        block = jnp.where(row < TOK, core, 1 - core)
        return landed_row(block)(row & (TOK - 1))

    return source


def back_kernel(where_ref, y_ref, own_ref, other_ref, *refs):
    arrays, (out_ref, whole_ref, weight, sems, rows) = refs[: len(PIECES)], refs[len(PIECES) :]
    more = [(own_ref, rows.at[0:TOK]), (other_ref, rows.at[TOK:])]
    assemble(where_ref, arrays, weight, sems, more)
    whole = pltpu.make_async_copy(weight, whole_ref, sems.at[len(PIECES) + 2])
    whole.start()
    width = y_ref.shape[1]
    out_ref[:, 0:width] = y_ref[...]
    for at, size in ((0, 256), (256, 256), (512, 128)):
        part = lax.dot_general(
            rows[...],
            weight[at : at + size, :],
            (((1,), (1,)), ((), ())),
            preferred_element_type=F32,
        ).astype(BF16)
        out_ref[:, width + at : width + at + size] = pick_rows(
            stacked_row(where_ref[1]), part.shape[0], part
        )
    whole.wait()


def back_rows(where, rows_y, own, other, arrays):
    columns = own.shape[1]
    return pl.pallas_call(
        back_kernel,
        out_shape=(
            jax.ShapeDtypeStruct((2 * TOK, 2 * NY * ROWS), BF16),
            jax.ShapeDtypeStruct((NY * ROWS, columns), BF16),
        ),
        in_specs=[SMEM, VMEM] + [AWAY] * (2 + len(arrays)),
        out_specs=(VMEM, AWAY),
        scratch_shapes=[
            pltpu.VMEM((NY * ROWS, columns), BF16),
            pltpu.SemaphoreType.DMA((len(PIECES) + 3,)),
            pltpu.VMEM((2 * TOK, columns), BF16),
        ],
        compiler_params=params(60 << 20),
    )(where, rows_y, own, other, *arrays)


def project_kernel(where_ref, landed_ref, whole_ref, keep_ref, send_ref, weight, sem):
    copy = pltpu.make_async_copy(whole_ref, weight, sem)
    copy.start()
    landed = landed_ref[:, 0 : weight.shape[0]]
    rows = pick_rows(both_rows(where_ref[1]), landed.shape[0], landed)
    copy.wait()
    for at in range(0, weight.shape[1], 768):
        part = jnp.dot(rows, weight[:, at : at + 768], preferred_element_type=F32)
        keep_ref[:, at : at + 768] = part[0:TOK]
        send_ref[:, at : at + 768] = part[TOK:]


def project(where, landed, whole):
    out = jax.ShapeDtypeStruct((TOK, whole.shape[1]), F32)
    return pl.pallas_call(
        project_kernel,
        out_shape=(out, out),
        in_specs=[SMEM, VMEM, AWAY],
        out_specs=(VMEM, VMEM),
        scratch_shapes=[pltpu.VMEM(whole.shape, BF16), pltpu.SemaphoreType.DMA],
        compiler_params=params(60 << 20),
        cost_estimate=pl.CostEstimate(
            flops=4 * TOK * whole.size, bytes_accessed=20_000_000, transcendentals=0
        ),
    )(where, landed, whole)


def chosen(channel_ref, width, dtype=BF16):
    shape = (width, channel_ref.shape[1])
    hit = lax.broadcasted_iota(jnp.int32, shape, 0) == channel_ref[...]
    return jnp.where(hit, 1.0, 0.0).astype(dtype)


def select_kernel(own_ref, other_ref, rows_ref, place_ref, kernel_ref, x_ref, send_ref, kern_ref):
    width = rows_ref.shape[1]
    mine = chosen(own_ref, width)
    x_ref[...] = jnp.dot(rows_ref[...], mine, preferred_element_type=F32).astype(BF16)
    theirs = chosen(other_ref, width)
    send_ref[0:TOK] = jnp.dot(rows_ref[...], theirs, preferred_element_type=F32).astype(BF16)
    send_ref[TOK:] = jnp.zeros((16, send_ref.shape[1]), BF16)
    place = jnp.broadcast_to(place_ref[...].astype(F32), (16, TOK)).astype(BF16)
    send_ref[TOK:, 0:TOK] = place
    kern_ref[...] = jnp.dot(
        kernel_ref[...],
        chosen(own_ref, width, F32),
        precision=lax.Precision.HIGHEST,
        preferred_element_type=F32,
    )


def put_cells(cell_ref, rows, out_ref, first_ref, last_ref):
    count = out_ref.shape[0]
    hit = lax.broadcasted_iota(jnp.int32, (count, count), 0) == cell_ref[...]
    cells = jnp.dot(one_hot(hit), rows, preferred_element_type=F32).astype(BF16)
    out_ref[...] = cells
    first_ref[...] = cells[0:LAYER]
    last_ref[...] = cells[count - LAYER :]


def join_kernel(cell_ref, own_ref, other_ref, *outs):
    put_cells(cell_ref, jnp.concatenate([own_ref[...], other_ref[0:TOK, :]], axis=0), *outs)


def cells_kernel(cell_ref, rows_ref, *outs):
    put_cells(cell_ref, rows_ref[:, rows_ref.shape[1] - outs[0].shape[1] :], *outs)


def in_vmem(body, out_shape, *operands, vmem=None, scalars=0):
    return pl.pallas_call(
        body,
        out_shape=out_shape,
        in_specs=[SMEM] * scalars + [VMEM] * (len(operands) - scalars),
        out_specs=jax.tree.map(lambda _: VMEM, out_shape),
        compiler_params=params(vmem),
    )(*operands)


def fill(before_ref, cells_ref, after_ref, field):
    lanes = cells_ref.shape[1]
    zero = jnp.zeros((6, 1, 8, lanes), F32)
    field[:, 0:1] = zero
    field[:, 9:10] = zero
    field[0:1, 1:9] = before_ref[...].astype(F32).reshape(1, 8, 8, lanes)
    field[1:5, 1:9] = cells_ref[...].astype(F32).reshape(4, 8, 8, lanes)
    field[5:6, 1:9] = after_ref[...].astype(F32).reshape(1, 8, 8, lanes)


def from_lower(value):
    column = lax.broadcasted_iota(jnp.int32, value.shape, value.ndim - 2)
    return jnp.where(column == 0, 0.0, jnp.roll(value, 1, axis=value.ndim - 2))


def from_upper(value):
    column = lax.broadcasted_iota(jnp.int32, value.shape, value.ndim - 2)
    return jnp.where(column == 7, 0.0, jnp.roll(value, -1, axis=value.ndim - 2))


def conv_body(flip, index_ref, kernel_ref, before_ref, cells_ref, after_ref, out_ref, field):
    fill(before_ref, cells_ref, after_ref, field)
    count, lanes = cells_ref.shape
    layers = []
    for z in range(4):
        sums = []
        for dc in range(3):
            total = None
            for o in range(dc, 27, 3):
                dz, di = o // 9, o // 3 % 3
                row = 26 - o if flip else o
                term = kernel_ref[row : row + 1, :][None] * field[z + dz, di : di + 8]
                total = term if total is None else total + term
            sums.append(total)
        layers.append(sums[1] + from_lower(sums[0]) + from_upper(sums[2]))
    conv = jnp.stack(layers).reshape(count, lanes)
    result = (cells_ref[...].astype(F32) + conv).astype(BF16)
    hit = lax.broadcasted_iota(jnp.int32, (count, count), 1) == index_ref[...]
    out_ref[...] = jnp.dot(one_hot(hit), result, preferred_element_type=F32).astype(BF16)


def high_part(value):
    return value.astype(BF16)


def rest_part(value):
    return (value - value.astype(BF16).astype(F32)).astype(BF16)


def back_conv_body(index_ref, kernel_ref, before_ref, cells_ref, after_ref, sums_ref, out_ref, field):
    step = pl.program_id(0)
    last = pl.num_programs(0) - 2

    @pl.when(step < last)
    def _():
        conv_body(True, index_ref, kernel_ref, before_ref, cells_ref, after_ref, out_ref, field)

    @pl.when(step == last)
    def _():
        out_ref[...] = high_part(sums_ref[...])

    @pl.when(step == last + 1)
    def _():
        out_ref[...] = rest_part(sums_ref[...])


def tall(rows, steps, lanes=128):
    return pl.BlockSpec((rows, lanes), lambda t: (0, jnp.minimum(t, steps - 1)))


def conv_rows(cells, before, after, kernel, cell_column, sums=None):
    count, width = cells.shape
    steps = width // 128
    specs = [
        pl.BlockSpec((count, 1), lambda t: (0, 0)),
        tall(kernel.shape[0], steps),
        tall(LAYER, steps),
        tall(count, steps),
        tall(LAYER, steps),
    ]
    operands = (cell_column, kernel, before, cells, after)
    if sums is not None:
        specs.append(pl.BlockSpec(sums.shape, lambda t: (0, 0)))
        operands += (sums,)
    wide = steps if sums is None else steps + 2
    return pl.pallas_call(
        functools.partial(conv_body, False) if sums is None else back_conv_body,
        out_shape=jax.ShapeDtypeStruct((count, wide * 128), BF16),
        grid=(wide,),
        in_specs=specs,
        out_specs=pl.BlockSpec((count, 128), lambda t: (0, t)),
        scratch_shapes=[pltpu.VMEM((6, 10, 8, 128), F32)],
    )(*operands)


def grad_body(steps, grad_ref, before_ref, cells_ref, after_ref, out_ref, field):
    @pl.when(pl.program_id(0) >= steps)
    def _():
        out_ref[...] = jnp.zeros_like(out_ref)

    @pl.when(pl.program_id(0) < steps)
    def _():
        fill(before_ref, cells_ref, after_ref, field)
        lanes = cells_ref.shape[1]
        grad = grad_ref[...].astype(F32).reshape(4, 8, 8, lanes)
        shifted = (from_upper(grad), grad, from_lower(grad))
        sums = []
        for o in range(27):
            dz, di, dc = o // 9, o // 3 % 3, o % 3
            part = shifted[dc] * field[dz : dz + 4, di : di + 8]
            sums.append(jnp.sum(part.reshape(32, 8, lanes), axis=0))
        sums += [jnp.zeros((8, lanes), F32)] * 5
        out_ref[...] = jnp.sum(jnp.stack(sums), axis=1)


def kernel_grad(grad, cells, before, after):
    count, width = cells.shape
    steps = width // 128
    return pl.pallas_call(
        functools.partial(grad_body, steps),
        out_shape=jax.ShapeDtypeStruct((count, 128), F32),
        grid=(count // 32,),
        in_specs=[tall(count, steps), tall(LAYER, steps), tall(count, steps), tall(LAYER, steps)],
        out_specs=pl.BlockSpec((32, 128), lambda t: (t, 0)),
        scratch_shapes=[pltpu.VMEM((6, 10, 8, 128), F32)],
    )(grad, before, cells, after)


def in_three(value):
    high = value.astype(BF16)
    rest = value - high.astype(F32)
    middle = rest.astype(BF16)
    low = (rest - middle.astype(F32)).astype(BF16)
    return jnp.concatenate([high, middle, low], axis=0)


def stack_parts(rows, tiles_ref):
    steps = NY * ROWS // 128
    tiles = [tiles_ref[4 * t : 4 * t + 4].reshape(32, 128) for t in range(steps)]
    return jnp.concatenate([rows, in_three(jnp.concatenate(tiles, axis=1))], axis=0)


def other_kernel(where_ref, landed_ref, out_ref):
    out_ref[...] = pick_rows(
        landed_row(1 - where_ref[1]), TOK, landed_ref[:, 0 : NY * ROWS]
    )


def last_kernel(where_ref, own_ch, other_ch, landed_ref, tiles_ref, rows_ref, other_ref, out_ref, grad_ref):
    width = out_ref.shape[1]
    contract = (((1,), (1,)), ((), ()))
    rows = pick_rows(landed_row(where_ref[1]), TOK, landed_ref[:, 0 : NY * ROWS])
    own = stack_parts(rows, tiles_ref)
    other = stack_parts(rows_ref[...], other_ref)
    total = lax.dot_general(own, chosen(own_ch, width), contract, preferred_element_type=F32)
    total = total + lax.dot_general(
        other, chosen(other_ch, width), contract, preferred_element_type=F32
    )
    out_ref[...] = total[0:TOK].astype(BF16)
    grad = total[TOK : TOK + 32] + total[TOK + 32 : TOK + 64] + total[TOK + 64 : TOK + 96]
    grad_ref[...] = grad[0 : grad_ref.shape[0]]


def landed_sum_kernel(landed_ref, out_ref):
    at = NY * ROWS
    parts = landed_ref[:, at : at + 128].astype(F32) + landed_ref[:, at + 128 : at + 256].astype(F32)
    total = jnp.sum(parts.reshape(CHIPS, 8, 128), axis=0)
    for i in range(out_ref.shape[0]):
        out_ref[i] = total


def sum_kernel(count, parts_ref, out_ref):
    total = parts_ref[0]
    for i in range(1, parts_ref.shape[0]):
        total = total + parts_ref[i]
    for i in range(count):
        out_ref[i] = total


def sum_spread(parts, axis, size):
    shape = jax.ShapeDtypeStruct((size, *parts.shape[1:]), F32)
    sent = in_vmem(functools.partial(sum_kernel, size), shape, parts)
    return lax.all_to_all(sent, axis, 0, 0, tiled=True)


def exchange(rows):
    count, width = rows.shape
    sent = rows.reshape(CHIPS, count // CHIPS, width)
    return lax.all_to_all(sent, ("y", "x"), 0, 0, tiled=True).reshape(count, width)


def faces(first, last):
    up = [(i, i + 1) for i in range(CHIPS - 1)]
    down = [(j, i) for i, j in up]
    return lax.ppermute(last, ("y", "x"), up), lax.ppermute(first, ("y", "x"), down)


def shards(planes, tokens, place, kernel, proj_weight, d_projected):
    core = lax.axis_index("c")
    where = jnp.stack([lax.axis_index("y"), core]).astype(jnp.int32)
    rows_x, rows_d = tokens[0], d_projected[0]
    width = rows_x.shape[1]
    local = width // NC

    other_d = swap(rows_d)
    block = after(spread(proj_weight, "x", NX), other_d).reshape(ROWS, proj_weight.shape[1])
    landed_x = exchange(after(rows_x, block))
    near = ring(block, block)
    second_near = ring(*near)

    steps = jnp.arange(local, dtype=jnp.int32)
    first = (steps // GROUP * (NC * GROUP) + steps % GROUP)[None]
    second = first + GROUP
    own_ch = jnp.where(core == 0, first, second)
    other_ch = jnp.where(core == 0, second, first)
    own_x, send_x, kern = in_vmem(
        select_kernel,
        (
            jax.ShapeDtypeStruct((TOK, local), BF16),
            jax.ShapeDtypeStruct((TOK + 16, local), BF16),
            jax.ShapeDtypeStruct((kernel.shape[0], local), F32),
        ),
        own_ch,
        other_ch,
        after(landed_x, *near),
        place,
        kernel,
        vmem=16 << 20,
    )
    other_x = swap(send_x)

    theirs = other_x[TOK, 0:TOK].astype(jnp.int32)
    places = jnp.stack([jnp.where(core == 0, place[0], theirs), jnp.where(core == 0, theirs, place[0])])
    cell = places.reshape(2, CHIPS, 2, 2) + jnp.array([0, TOK], jnp.int32)[:, None, None, None]
    by_block = cell.transpose(2, 1, 0, 3).reshape(2, TOK)
    stacked = jnp.where(core == 0, by_block, by_block[::-1]).reshape(1, 2 * TOK)
    cell = cell.transpose(1, 2, 0, 3).reshape(2 * TOK)
    cell_row, cell_column = cell[None, :], cell[:, None]

    layer = jax.ShapeDtypeStruct((LAYER, local), BF16)
    pair = (jax.ShapeDtypeStruct((2 * TOK, local), BF16), layer, layer)
    third_near = ring(*lax.optimization_barrier((*second_near, own_x))[:2])
    cells_x, first_x, last_x = in_vmem(join_kernel, pair, stacked, own_x, other_x)
    before_x, after_x = faces(first_x, last_x)
    up, down, before_x, after_x = lax.optimization_barrier((*third_near, before_x, after_x))
    far = (shift(up[:CUT], "y", NY, 1), shift(down[CUT:], "y", NY, -1))
    rows_y = conv_rows(cells_x, before_x, after_x, kern, cell_column)

    arrays = (block, *near, *second_near, *third_near, *far)
    sent, whole = back_rows(where, rows_y, rows_d, other_d, arrays)
    landed = exchange(sent)
    cells_d, first_d, last_d = in_vmem(cells_kernel, pair, cell_row, landed)
    before_d, after_d = faces(first_d, last_d)
    sums = kernel_grad(cells_d, cells_x, before_x, after_x)
    back = conv_rows(cells_d, before_d, after_d, kern, cell_column, sums)
    landed = after(landed, back)
    keep, send = project(where, landed, whole)
    landed_d, keep = lax.optimization_barrier((exchange(back), keep))
    tile = jax.ShapeDtypeStruct((planes, 8, 128), F32)
    tiles = lax.all_to_all(in_vmem(landed_sum_kernel, tile, landed_d), "z", 0, 0, tiled=True)
    send, landed_d = lax.optimization_barrier((send, landed_d, tiles))[:2]
    tiles = sum_spread(tiles, ("y", "x"), CHIPS)
    other_rows = jax.ShapeDtypeStruct((TOK, local), BF16)
    d_other = swap(in_vmem(other_kernel, other_rows, where, landed_d, scalars=1))
    projected = (keep + swap(send)).astype(BF16)
    tiles, projected, d_other = lax.optimization_barrier((tiles, projected, d_other))

    d_tokens, d_kernel = in_vmem(
        last_kernel,
        (
            jax.ShapeDtypeStruct((TOK, width), BF16),
            jax.ShapeDtypeStruct(kernel.shape, F32),
        ),
        where,
        own_ch,
        other_ch,
        landed_d,
        tiles,
        d_other,
        swap(tiles),
        vmem=16 << 20,
        scalars=1,
    )
    return projected[None], d_tokens[None], d_kernel


def solution(mesh):
    planes = mesh.shape["dp"]
    devices = np.asarray(mesh.devices).reshape(planes, NY, NX, NC)
    grid = Mesh(devices, ("z", "y", "x", "c"))
    seq = ("y", "x", "c")
    return jax.shard_map(
        functools.partial(shards, planes),
        mesh=grid,
        in_specs=(P("z", seq, None), P(seq, None), P(), P(seq, None), P("z", seq, None)),
        out_specs=(P("z", seq, None), P("z", seq, None), P()),
        check_vma=False,
    )
```

```python
import functools

import jax
import jax.numpy as jnp
import numpy as np
from jax import lax
from jax.experimental import pallas as pl
from jax.experimental.pallas import tpu as pltpu
from jax.sharding import Mesh
from jax.sharding import PartitionSpec as P

NY, NX, NC = 8, 4, 2
CHIPS = NY * NX
TOK = 128
LAYER = 64
GROUP = 20
BF16, F32 = jnp.bfloat16, jnp.float32
VMEM = pl.BlockSpec(memory_space=pltpu.VMEM)
SMEM = pl.BlockSpec(memory_space=pltpu.SMEM)
AWAY = pl.BlockSpec(memory_space=pltpu.HBM)


def swap(value):
    return lax.ppermute(value, "c", [(0, 1), (1, 0)])


def spread(value, axis, size):
    return lax.all_to_all(
        jnp.broadcast_to(value[None], (size, *value.shape)), axis, 0, 0, tiled=True
    )


def shift(value, axis, size, step):
    return lax.ppermute(value, axis, [(i, (i + step) % size) for i in range(size)])


def after(value, *others):
    return lax.optimization_barrier((value, *others))[0]


def params(vmem=None):
    return pltpu.CompilerParams(vmem_limit_bytes=vmem)


ROWS = NX * GROUP
CUT = 48
PIECES = [(s, 0, ROWS) for s in (0, -1, 1, -2, 2, -3, 3)] + [(4, 0, CUT), (4, CUT, ROWS - CUT)]


def ring(up, down):
    return shift(up, "y", NY, 1), shift(down, "y", NY, -1)


def assemble(where_ref, arrays, weight, sems, more):
    copies = [
        pltpu.make_async_copy(source, target, sems.at[len(PIECES) + i])
        for i, (source, target) in enumerate(more)
    ]
    for i, (step, skip, rows) in enumerate(PIECES):
        row = pl.multiple_of(lax.rem(where_ref[0] + step + NY, NY) * ROWS + skip, 16)
        copies.append(
            pltpu.make_async_copy(arrays[i], weight.at[pl.ds(row, rows)], sems.at[i])
        )
    for copy in copies:
        copy.start()
    for copy in copies:
        copy.wait()


def one_hot(hit):
    return jnp.where(hit, 1.0, 0.0).astype(BF16)


def pick_rows(source, count, value):
    shape = (count, value.shape[0])
    hit = lax.broadcasted_iota(jnp.int32, shape, 1) == source(
        lax.broadcasted_iota(jnp.int32, shape, 0)
    )
    return jnp.dot(one_hot(hit), value, preferred_element_type=F32).astype(BF16)


def stacked_row(core):
    def source(row):
        block = lax.shift_right_logical(row, 2) & 1
        at = lax.shift_left(lax.shift_right_logical(row, 3), 2) + (row & 3)
        return at + jnp.where(block == core, 0, TOK)

    return source


def landed_row(block):
    def source(row):
        return lax.shift_left(lax.shift_right_logical(row, 2), 3) + (row & 3) + block * 4

    return source


def both_rows(core):
    def source(row):
        block = jnp.where(row < TOK, core, 1 - core)
        return landed_row(block)(row & (TOK - 1))

    return source


def back_kernel(where_ref, y_ref, own_ref, other_ref, *refs):
    arrays, (out_ref, whole_ref, weight, sems, rows) = refs[: len(PIECES)], refs[len(PIECES) :]
    more = [(own_ref, rows.at[0:TOK]), (other_ref, rows.at[TOK:])]
    assemble(where_ref, arrays, weight, sems, more)
    whole = pltpu.make_async_copy(weight, whole_ref, sems.at[len(PIECES) + 2])
    whole.start()
    width = y_ref.shape[1]
    out_ref[:, 0:width] = y_ref[...]
    for at, size in ((0, 256), (256, 256), (512, 128)):
        part = lax.dot_general(
            rows[...],
            weight[at : at + size, :],
            (((1,), (1,)), ((), ())),
            preferred_element_type=F32,
        ).astype(BF16)
        out_ref[:, width + at : width + at + size] = pick_rows(
            stacked_row(where_ref[1]), part.shape[0], part
        )
    whole.wait()


def back_rows(where, rows_y, own, other, arrays):
    columns = own.shape[1]
    return pl.pallas_call(
        back_kernel,
        out_shape=(
            jax.ShapeDtypeStruct((2 * TOK, 2 * NY * ROWS), BF16),
            jax.ShapeDtypeStruct((NY * ROWS, columns), BF16),
        ),
        in_specs=[SMEM, VMEM] + [AWAY] * (2 + len(arrays)),
        out_specs=(VMEM, AWAY),
        scratch_shapes=[
            pltpu.VMEM((NY * ROWS, columns), BF16),
            pltpu.SemaphoreType.DMA((len(PIECES) + 3,)),
            pltpu.VMEM((2 * TOK, columns), BF16),
        ],
        compiler_params=params(60 << 20),
    )(where, rows_y, own, other, *arrays)


def project_kernel(where_ref, landed_ref, whole_ref, keep_ref, send_ref, weight, sem):
    copy = pltpu.make_async_copy(whole_ref, weight, sem)
    copy.start()
    landed = landed_ref[:, 0 : weight.shape[0]]
    rows = pick_rows(both_rows(where_ref[1]), landed.shape[0], landed)
    copy.wait()
    for at in range(0, weight.shape[1], 768):
        part = jnp.dot(rows, weight[:, at : at + 768], preferred_element_type=F32)
        keep_ref[:, at : at + 768] = part[0:TOK]
        send_ref[:, at : at + 768] = part[TOK:]


def project(where, landed, whole):
    out = jax.ShapeDtypeStruct((TOK, whole.shape[1]), F32)
    return pl.pallas_call(
        project_kernel,
        out_shape=(out, out),
        in_specs=[SMEM, VMEM, AWAY],
        out_specs=(VMEM, VMEM),
        scratch_shapes=[pltpu.VMEM(whole.shape, BF16), pltpu.SemaphoreType.DMA],
        compiler_params=params(60 << 20),
        cost_estimate=pl.CostEstimate(
            flops=4 * TOK * whole.size, bytes_accessed=20_000_000, transcendentals=0
        ),
    )(where, landed, whole)


def chosen(channel_ref, width, dtype=BF16):
    shape = (width, channel_ref.shape[1])
    hit = lax.broadcasted_iota(jnp.int32, shape, 0) == channel_ref[...]
    return jnp.where(hit, 1.0, 0.0).astype(dtype)


def select_kernel(own_ref, other_ref, rows_ref, place_ref, kernel_ref, x_ref, send_ref, kern_ref):
    width = rows_ref.shape[1]
    mine = chosen(own_ref, width)
    x_ref[...] = jnp.dot(rows_ref[...], mine, preferred_element_type=F32).astype(BF16)
    theirs = chosen(other_ref, width)
    send_ref[0:TOK] = jnp.dot(rows_ref[...], theirs, preferred_element_type=F32).astype(BF16)
    send_ref[TOK:] = jnp.zeros((16, send_ref.shape[1]), BF16)
    place = jnp.broadcast_to(place_ref[...].astype(F32), (16, TOK)).astype(BF16)
    send_ref[TOK:, 0:TOK] = place
    kern_ref[...] = jnp.dot(
        kernel_ref[...],
        chosen(own_ref, width, F32),
        precision=lax.Precision.HIGHEST,
        preferred_element_type=F32,
    )


def put_cells(cell_ref, rows, out_ref, first_ref, last_ref):
    count = out_ref.shape[0]
    hit = lax.broadcasted_iota(jnp.int32, (count, count), 0) == cell_ref[...]
    cells = jnp.dot(one_hot(hit), rows, preferred_element_type=F32).astype(BF16)
    out_ref[...] = cells
    first_ref[...] = cells[0:LAYER]
    last_ref[...] = cells[count - LAYER :]


def join_kernel(cell_ref, own_ref, other_ref, *outs):
    put_cells(cell_ref, jnp.concatenate([own_ref[...], other_ref[0:TOK, :]], axis=0), *outs)


def cells_kernel(cell_ref, rows_ref, *outs):
    put_cells(cell_ref, rows_ref[:, rows_ref.shape[1] - outs[0].shape[1] :], *outs)


def in_vmem(body, out_shape, *operands, vmem=None, scalars=0):
    return pl.pallas_call(
        body,
        out_shape=out_shape,
        in_specs=[SMEM] * scalars + [VMEM] * (len(operands) - scalars),
        out_specs=jax.tree.map(lambda _: VMEM, out_shape),
        compiler_params=params(vmem),
    )(*operands)


def fill(before_ref, cells_ref, after_ref, field):
    lanes = cells_ref.shape[1]
    zero = jnp.zeros((6, 1, 8, lanes), F32)
    field[:, 0:1] = zero
    field[:, 9:10] = zero
    field[0:1, 1:9] = before_ref[...].astype(F32).reshape(1, 8, 8, lanes)
    field[1:5, 1:9] = cells_ref[...].astype(F32).reshape(4, 8, 8, lanes)
    field[5:6, 1:9] = after_ref[...].astype(F32).reshape(1, 8, 8, lanes)


def from_lower(value):
    column = lax.broadcasted_iota(jnp.int32, value.shape, value.ndim - 2)
    return jnp.where(column == 0, 0.0, jnp.roll(value, 1, axis=value.ndim - 2))


def from_upper(value):
    column = lax.broadcasted_iota(jnp.int32, value.shape, value.ndim - 2)
    return jnp.where(column == 7, 0.0, jnp.roll(value, -1, axis=value.ndim - 2))


def conv_body(flip, index_ref, kernel_ref, before_ref, cells_ref, after_ref, out_ref, field):
    fill(before_ref, cells_ref, after_ref, field)
    count, lanes = cells_ref.shape
    layers = []
    for z in range(4):
        sums = []
        for dc in range(3):
            total = None
            for o in range(dc, 27, 3):
                dz, di = o // 9, o // 3 % 3
                row = 26 - o if flip else o
                term = kernel_ref[row : row + 1, :][None] * field[z + dz, di : di + 8]
                total = term if total is None else total + term
            sums.append(total)
        layers.append(sums[1] + from_lower(sums[0]) + from_upper(sums[2]))
    conv = jnp.stack(layers).reshape(count, lanes)
    result = (cells_ref[...].astype(F32) + conv).astype(BF16)
    hit = lax.broadcasted_iota(jnp.int32, (count, count), 1) == index_ref[...]
    out_ref[...] = jnp.dot(one_hot(hit), result, preferred_element_type=F32).astype(BF16)


def high_part(value):
    return value.astype(BF16)


def rest_part(value):
    return (value - value.astype(BF16).astype(F32)).astype(BF16)


def back_conv_body(index_ref, kernel_ref, before_ref, cells_ref, after_ref, sums_ref, out_ref, field):
    step = pl.program_id(0)
    last = pl.num_programs(0) - 2

    @pl.when(step < last)
    def _():
        conv_body(True, index_ref, kernel_ref, before_ref, cells_ref, after_ref, out_ref, field)

    @pl.when(step == last)
    def _():
        out_ref[...] = high_part(sums_ref[...])

    @pl.when(step == last + 1)
    def _():
        out_ref[...] = rest_part(sums_ref[...])


def tall(rows, steps, lanes=128):
    return pl.BlockSpec((rows, lanes), lambda t: (0, jnp.minimum(t, steps - 1)))


def conv_rows(cells, before, after, kernel, cell_column, sums=None):
    count, width = cells.shape
    steps = width // 128
    specs = [
        pl.BlockSpec((count, 1), lambda t: (0, 0)),
        tall(kernel.shape[0], steps),
        tall(LAYER, steps),
        tall(count, steps),
        tall(LAYER, steps),
    ]
    operands = (cell_column, kernel, before, cells, after)
    if sums is not None:
        specs.append(pl.BlockSpec(sums.shape, lambda t: (0, 0)))
        operands += (sums,)
    wide = steps if sums is None else steps + 2
    return pl.pallas_call(
        functools.partial(conv_body, False) if sums is None else back_conv_body,
        out_shape=jax.ShapeDtypeStruct((count, wide * 128), BF16),
        grid=(wide,),
        in_specs=specs,
        out_specs=pl.BlockSpec((count, 128), lambda t: (0, t)),
        scratch_shapes=[pltpu.VMEM((6, 10, 8, 128), F32)],
    )(*operands)


def grad_body(steps, grad_ref, before_ref, cells_ref, after_ref, out_ref, field):
    @pl.when(pl.program_id(0) >= steps)
    def _():
        out_ref[...] = jnp.zeros_like(out_ref)

    @pl.when(pl.program_id(0) < steps)
    def _():
        fill(before_ref, cells_ref, after_ref, field)
        lanes = cells_ref.shape[1]
        grad = grad_ref[...].astype(F32).reshape(4, 8, 8, lanes)
        shifted = (from_upper(grad), grad, from_lower(grad))
        sums = []
        for o in range(27):
            dz, di, dc = o // 9, o // 3 % 3, o % 3
            part = shifted[dc] * field[dz : dz + 4, di : di + 8]
            sums.append(jnp.sum(part.reshape(32, 8, lanes), axis=0))
        sums += [jnp.zeros((8, lanes), F32)] * 5
        out_ref[...] = jnp.sum(jnp.stack(sums), axis=1)


def kernel_grad(grad, cells, before, after):
    count, width = cells.shape
    steps = width // 128
    return pl.pallas_call(
        functools.partial(grad_body, steps),
        out_shape=jax.ShapeDtypeStruct((count, 128), F32),
        grid=(count // 32,),
        in_specs=[tall(count, steps), tall(LAYER, steps), tall(count, steps), tall(LAYER, steps)],
        out_specs=pl.BlockSpec((32, 128), lambda t: (t, 0)),
        scratch_shapes=[pltpu.VMEM((6, 10, 8, 128), F32)],
    )(grad, before, cells, after)


def in_three(value):
    high = value.astype(BF16)
    rest = value - high.astype(F32)
    middle = rest.astype(BF16)
    low = (rest - middle.astype(F32)).astype(BF16)
    return jnp.concatenate([high, middle, low], axis=0)


def stack_parts(rows, tiles_ref):
    steps = NY * ROWS // 128
    tiles = [tiles_ref[4 * t : 4 * t + 4].reshape(32, 128) for t in range(steps)]
    return jnp.concatenate([rows, in_three(jnp.concatenate(tiles, axis=1))], axis=0)


def other_kernel(where_ref, landed_ref, out_ref):
    out_ref[...] = pick_rows(
        landed_row(1 - where_ref[1]), TOK, landed_ref[:, 0 : NY * ROWS]
    )


def last_kernel(where_ref, own_ch, other_ch, landed_ref, tiles_ref, rows_ref, other_ref, out_ref, grad_ref):
    width = out_ref.shape[1]
    contract = (((1,), (1,)), ((), ()))
    rows = pick_rows(landed_row(where_ref[1]), TOK, landed_ref[:, 0 : NY * ROWS])
    own = stack_parts(rows, tiles_ref)
    other = stack_parts(rows_ref[...], other_ref)
    total = lax.dot_general(own, chosen(own_ch, width), contract, preferred_element_type=F32)
    total = total + lax.dot_general(
        other, chosen(other_ch, width), contract, preferred_element_type=F32
    )
    out_ref[...] = total[0:TOK].astype(BF16)
    grad = total[TOK : TOK + 32] + total[TOK + 32 : TOK + 64] + total[TOK + 64 : TOK + 96]
    grad_ref[...] = grad[0 : grad_ref.shape[0]]


def landed_sum_kernel(landed_ref, out_ref):
    at = NY * ROWS
    parts = landed_ref[:, at : at + 128].astype(F32) + landed_ref[:, at + 128 : at + 256].astype(F32)
    total = jnp.sum(parts.reshape(CHIPS, 8, 128), axis=0)
    for i in range(out_ref.shape[0]):
        out_ref[i] = total


def sum_kernel(count, parts_ref, out_ref):
    total = parts_ref[0]
    for i in range(1, parts_ref.shape[0]):
        total = total + parts_ref[i]
    for i in range(count):
        out_ref[i] = total


def sum_spread(parts, axis, size):
    shape = jax.ShapeDtypeStruct((size, *parts.shape[1:]), F32)
    sent = in_vmem(functools.partial(sum_kernel, size), shape, parts)
    return lax.all_to_all(sent, axis, 0, 0, tiled=True)


def exchange(rows):
    count, width = rows.shape
    sent = rows.reshape(CHIPS, count // CHIPS, width)
    return lax.all_to_all(sent, ("y", "x"), 0, 0, tiled=True).reshape(count, width)


def faces(first, last):
    up = [(i, i + 1) for i in range(CHIPS - 1)]
    down = [(j, i) for i, j in up]
    return lax.ppermute(last, ("y", "x"), up), lax.ppermute(first, ("y", "x"), down)


def shards(planes, tokens, place, kernel, proj_weight, d_projected):
    core = lax.axis_index("c")
    where = jnp.stack([lax.axis_index("y"), core]).astype(jnp.int32)
    rows_x, rows_d = tokens[0], d_projected[0]
    width = rows_x.shape[1]
    local = width // NC

    block = spread(proj_weight, "x", NX).reshape(ROWS, proj_weight.shape[1])
    landed_x = exchange(after(rows_x, block))
    near = ring(block, block)
    second_near = ring(*near)

    steps = jnp.arange(local, dtype=jnp.int32)
    first = (steps // GROUP * (NC * GROUP) + steps % GROUP)[None]
    second = first + GROUP
    own_ch = jnp.where(core == 0, first, second)
    other_ch = jnp.where(core == 0, second, first)
    own_x, send_x, kern = in_vmem(
        select_kernel,
        (
            jax.ShapeDtypeStruct((TOK, local), BF16),
            jax.ShapeDtypeStruct((TOK + 16, local), BF16),
            jax.ShapeDtypeStruct((kernel.shape[0], local), F32),
        ),
        own_ch,
        other_ch,
        after(landed_x, *near),
        place,
        kernel,
        vmem=16 << 20,
    )
    other_x = swap(send_x)

    theirs = other_x[TOK, 0:TOK].astype(jnp.int32)
    places = jnp.stack([jnp.where(core == 0, place[0], theirs), jnp.where(core == 0, theirs, place[0])])
    cell = places.reshape(2, CHIPS, 2, 2) + jnp.array([0, TOK], jnp.int32)[:, None, None, None]
    by_block = cell.transpose(2, 1, 0, 3).reshape(2, TOK)
    stacked = jnp.where(core == 0, by_block, by_block[::-1]).reshape(1, 2 * TOK)
    cell = cell.transpose(1, 2, 0, 3).reshape(2 * TOK)
    cell_row, cell_column = cell[None, :], cell[:, None]

    layer = jax.ShapeDtypeStruct((LAYER, local), BF16)
    pair = (jax.ShapeDtypeStruct((2 * TOK, local), BF16), layer, layer)
    other_d = swap(after(rows_d, landed_x))
    *second_near, own_x, other_d = lax.optimization_barrier((*second_near, own_x, other_d))
    third_near = ring(*second_near)
    cells_x, first_x, last_x = in_vmem(join_kernel, pair, stacked, own_x, other_x)
    before_x, after_x = faces(first_x, last_x)
    up, down, before_x, after_x = lax.optimization_barrier((*third_near, before_x, after_x))
    far = (shift(up[:CUT], "y", NY, 1), shift(down[CUT:], "y", NY, -1))
    rows_y = conv_rows(cells_x, before_x, after_x, kern, cell_column)

    arrays = (block, *near, *second_near, *third_near, *far)
    sent, whole = back_rows(where, rows_y, rows_d, other_d, arrays)
    landed = exchange(sent)
    cells_d, first_d, last_d = in_vmem(cells_kernel, pair, cell_row, landed)
    before_d, after_d = faces(first_d, last_d)
    sums = kernel_grad(cells_d, cells_x, before_x, after_x)
    back = conv_rows(cells_d, before_d, after_d, kern, cell_column, sums)
    landed = after(landed, back)
    keep, send = project(where, landed, whole)
    landed_d, keep = lax.optimization_barrier((exchange(back), keep))
    tile = jax.ShapeDtypeStruct((planes, 8, 128), F32)
    tiles = lax.all_to_all(in_vmem(landed_sum_kernel, tile, landed_d), "z", 0, 0, tiled=True)
    send, landed_d = lax.optimization_barrier((send, landed_d, tiles))[:2]
    tiles = sum_spread(tiles, ("y", "x"), CHIPS)
    other_rows = jax.ShapeDtypeStruct((TOK, local), BF16)
    d_other = swap(in_vmem(other_kernel, other_rows, where, landed_d, scalars=1))
    projected = (keep + swap(send)).astype(BF16)
    tiles, projected, d_other = lax.optimization_barrier((tiles, projected, d_other))

    d_tokens, d_kernel = in_vmem(
        last_kernel,
        (
            jax.ShapeDtypeStruct((TOK, width), BF16),
            jax.ShapeDtypeStruct(kernel.shape, F32),
        ),
        where,
        own_ch,
        other_ch,
        landed_d,
        tiles,
        d_other,
        swap(tiles),
        vmem=16 << 20,
        scalars=1,
    )
    return projected[None], d_tokens[None], d_kernel


def solution(mesh):
    planes = mesh.shape["dp"]
    devices = np.asarray(mesh.devices).reshape(planes, NY, NX, NC)
    grid = Mesh(devices, ("z", "y", "x", "c"))
    seq = ("y", "x", "c")
    return jax.shard_map(
        functools.partial(shards, planes),
        mesh=grid,
        in_specs=(P("z", seq, None), P(seq, None), P(), P(seq, None), P("z", seq, None)),
        out_specs=(P("z", seq, None), P("z", seq, None), P()),
        check_vma=False,
    )
```
